32 devices in a mesh: dp: 4 (over z), expert: 8 (over y, x, core).
Axes of the slice: x: 2, y: 2, z: 4, core: 2. Of those that a mesh axis runs over, the one named last changes fastest.
Arguments:
- out_grad: bfloat16 [4096, 1440], P(('dp', 'expert')), may hold values from -0.119628906 to 0.119628906
- expert_ids: int32 [4096, 4], P(('dp', 'expert')), may hold values from 0 to 7, all different within a row; in each aligned block of 128 rows (0 to 127, 128 to 255, ...) at most 64 rows name the same one
- gate_weight: float32 [4096, 4], P(('dp', 'expert')), may hold values from 0.1 to 1
- saved_hidden: bfloat16 [4, 8, 8, 64, 1440], P('dp', 'expert'), may hold values from -6 to 6
- saved_output: bfloat16 [4, 8, 8, 64, 1440], P('dp', 'expert'), may hold values from -6 to 6
Outputs:
- down_grad: bfloat16 [8, 1440, 1440], P('expert', 'dp')
- route_grad: float32 [4096, 4], P(('dp', 'expert'))
The draws below stay inside these ranges and needn't reach their ends.
Inputs may be any that keep to these rules, and one draw needn't show every extreme that they name: `expert_ids`: among the 128 tokens of one device each expert is named by at most 64 of the top-4 choices, a bound that some block reaches; a token names 4 different experts.
All inputs are finite; a program needn't handle non-finite values.
Results may differ from the reference program's by a relative error of at most 0.015.
Values may be sent and summed in bfloat16 or wider, within the bound.
No kernel may reach another device: no remote copies, remote signals or barrier semaphores. Data moves between devices by JAX's collectives and lax.ppermute only.
A program may use at most 64 MiB of HBM per device.

```python
import math
import jax
import jax.numpy as jnp
import numpy as np
from jax import lax

D = 1440
FF = 1440
TOP = 4
TOK_DEV = 128
EXPERTS = 8
SOURCES = 8
GROUPS = 4
CAP = 64
TOKENS = 4096


def with_spikes(drawn, own_key, source, target, blocks, factor):
    def block_of(dim):
        return (jnp.arange(drawn.shape[dim]) // (drawn.shape[dim] // blocks)).reshape((-1,) + (1,) * (drawn.ndim - 1 - dim))

    near = jax.random.permutation(own_key, blocks)[block_of(target)]
    other_side = (block_of(target) + blocks // 2) % blocks
    return jnp.where((block_of(source) == near) | (block_of(source) == other_side), factor * drawn, drawn)


def shard_levels(key, extent, shards, smallest, largest):
    def one(dim, blocks):
        steps = jax.random.uniform(jax.random.fold_in(jax.random.fold_in(key, 6), dim), (blocks,), jnp.float32, smallest / len(shards), largest / len(shards))
        return jnp.repeat(jnp.exp(steps), extent[dim] // blocks).reshape((-1,) + (1,) * (len(extent) - dim - 1))

    level = one(*shards[0])
    for cut in shards[1:]:
        level = level * one(*cut)
    return level


def assign_block(key, own, number, rows, number_of, top, limit, slope):
    order = jax.random.permutation(key, number_of)
    heavy_load, ordinary = load_shares(number_of, rows * top, limit, slope, True), load_shares(number_of, rows * top, limit, slope, False)
    places = jnp.arange(number_of)

    def named(sizes, turn):
        used = int((sizes > 0).sum())
        fixed = max(1, used // 4)
        passed = fixed + (places - fixed + turn * (used - fixed)) % max(1, number_of - fixed)
        return jnp.zeros((number_of,), jnp.int32).at[order[jnp.where(places < fixed, places, passed)]].set(jnp.asarray(sizes, jnp.int32))

    sizes = jnp.where(number % 4 == 0, named(heavy_load, number // 4), named(ordinary, number - number // 4 - 1))
    mixed = jax.random.permutation(jax.random.fold_in(own, 3), number_of)
    donor, sink = mixed[0:number_of // 2 * 2:2], mixed[1:number_of // 2 * 2:2]
    margin = jnp.minimum(sizes[donor] - 1, limit - sizes[sink]) // 2
    margin = jnp.where((donor == order[0]) | (sink == order[0]) | (sizes[sink] == 0), 0, jnp.maximum(margin, 0))
    passed = jax.random.randint(jax.random.fold_in(own, 4), (number_of // 2,), 0, 1 << 20) % (margin + 1)
    sizes = sizes.at[donor].add(-passed).at[sink].add(passed)
    labels = jnp.searchsorted(jnp.cumsum(sizes), jnp.arange(rows * top), side="right").astype(jnp.int32)
    table = labels.reshape(top, rows).T
    table = table[jax.random.permutation(jax.random.fold_in(own, 1), rows)]
    turn = jax.random.randint(jax.random.fold_in(own, 2), (rows, 1), 0, top)
    return jnp.take_along_axis(table, (jnp.arange(top)[None, :] + turn) % top, axis=1)


def load_shares(amount, total, most, skew, full):
    weights = [(1 << 20) // math.isqrt(rank ** skew) + 1 for rank in range(1, amount + 1)]
    largest = most if full else min(most, max(-(-total // amount), total * weights[0] // sum(weights)))
    least = 1 if total - largest >= amount - 1 else 0
    counts, rest = [largest] + [least] * (amount - 1), total - largest - least * (amount - 1)
    while rest > 0:
        candidates = [i for i in range(1, amount) if counts[i] < largest] or [i for i in range(1, amount) if counts[i] < most]
        whole, remaining = sum([weights[i] for i in candidates]), rest
        for i in candidates:
            addition = min(most - counts[i], max(1, remaining * weights[i] // whole), rest)
            counts[i] = counts[i] + addition
            rest = rest - addition
    return np.array(counts)


def bell_draw(stream_key, extent, scale, bound, pieces=(), kind=jnp.bfloat16):
    entries = scale * jax.random.normal(stream_key, extent, jnp.float32)
    if pieces:
        entries = entries * shard_levels(stream_key, extent, pieces, -0.22, 0.18)
    return jnp.clip(entries, -bound, bound).astype(kind)


def gaussian_with(rng, dims, spread, limit, cuts, heavy, kind=jnp.bfloat16):
    entries = spread * jax.random.normal(rng, dims, jnp.float32)
    if cuts:
        entries = entries * shard_levels(rng, dims, cuts, -0.22, 0.18)
    return jnp.clip(with_spikes(entries, jax.random.fold_in(rng, 3), *heavy), -limit, limit).astype(kind)


def setup_inputs(seed: int = 0) -> dict:
    key_list = jax.random.split(jax.random.key(seed), 6)
    out_grad = bell_draw(key_list[0], (TOKENS, D), 0.02, 0.119628906, ((0, 32),))
    expert_ids_keys = jax.random.split(jax.random.fold_in(key_list[1], 1), TOKENS // TOK_DEV)
    expert_ids_turns = jax.random.permutation(jax.random.fold_in(key_list[1], 3), TOKENS // TOK_DEV)
    expert_ids = jax.vmap(lambda own, number: assign_block(jax.random.fold_in(key_list[1], 2), own, number, TOK_DEV, EXPERTS, TOP, CAP, 0))(expert_ids_keys, expert_ids_turns).reshape((TOKENS, TOP))
    gate_weight = jnp.clip(0.1 + 0.9 * jax.random.uniform(key_list[2], (TOKENS, TOP), jnp.float32) ** shard_levels(key_list[2], (TOKENS, TOP), ((0, 32),), -0.2, 0.2), 0.1, 1.0)
    saved_hidden = gaussian_with(key_list[3], (GROUPS, EXPERTS, SOURCES, CAP, FF), 1.0, 6.0, ((0, 4), (1, 8)), (0, 4, 4, 2.0))
    saved_output = bell_draw(key_list[4], (GROUPS, EXPERTS, SOURCES, CAP, D), 1.0, 6.0, ((0, 4), (1, 8)))
    return dict(out_grad=out_grad, expert_ids=expert_ids, gate_weight=gate_weight, saved_hidden=saved_hidden, saved_output=saved_output)


def slot_numbers(ids, experts, capacity):
    rows = ids.shape[0] * ids.shape[1]
    flat = (ids.reshape(rows, 1) == jnp.arange(experts, dtype=jnp.int32)[None, :]).astype(jnp.int32)
    earlier = jnp.cumsum(flat, axis=0) - flat
    position = jnp.sum(earlier * flat, axis=1).reshape(ids.shape)
    return (ids * capacity + position).astype(jnp.int32)


def dispatch_block(grad_rows, ids, gates):
    slot = slot_numbers(ids, EXPERTS, CAP)
    table = slot[:, :, None] == jnp.arange(EXPERTS * CAP, dtype=jnp.int32)[None, None, :]
    occupancy = jnp.sum(table, axis=1).astype(jnp.bfloat16)
    sent = lax.dot_general(occupancy, grad_rows, (((0,), (0,)), ((), ())), preferred_element_type=jnp.float32)
    gate_slots = jnp.sum(jnp.where(table, gates[:, :, None], jnp.float32(0.0)), axis=(0, 1))
    scaled = (gate_slots[:, None] * sent).astype(jnp.bfloat16)
    return scaled.reshape(EXPERTS, CAP, D)


def reference(out_grad, expert_ids, gate_weight, saved_hidden, saved_output):
    grad_blocks = out_grad.reshape(GROUPS, SOURCES, TOK_DEV, D)
    id_blocks = expert_ids.reshape(GROUPS, SOURCES, TOK_DEV, TOP)
    gate_blocks = gate_weight.reshape(GROUPS, SOURCES, TOK_DEV, TOP)

    def group_step(total, group):
        scaled = jax.vmap(dispatch_block)(grad_blocks[group], id_blocks[group], gate_blocks[group])
        hidden = saved_hidden[group].astype(jnp.float32)
        partial_value = jnp.einsum("escf,secd->efd", hidden, scaled.astype(jnp.float32))
        return total + partial_value.astype(jnp.bfloat16).astype(jnp.float32), None

    start = jnp.zeros((EXPERTS, FF, D), jnp.float32)
    down_grad, unused = lax.scan(group_step, start, jnp.arange(GROUPS, dtype=jnp.int32))

    def block_score(index):
        group = index // SOURCES
        source = index % SOURCES
        ids = id_blocks[group, source]
        slot = slot_numbers(ids, EXPERTS, CAP)
        position = slot - ids * CAP
        picked = saved_output[group][ids, source, position]
        return jnp.einsum("tkd,td->tk", picked.astype(jnp.float32), grad_blocks[group, source].astype(jnp.float32))

    scores = lax.map(block_score, jnp.arange(GROUPS * SOURCES, dtype=jnp.int32))
    return down_grad.astype(jnp.bfloat16), scores.reshape(TOKENS, TOP)
```

```python
import functools

import jax
import jax.numpy as jnp
from jax import lax
from jax.experimental import pallas as pl
from jax.experimental.pallas import tpu as pltpu
from jax.sharding import PartitionSpec as P

LANES = 128
META = 16


def slot_numbers(ids, experts, capacity):
    rows = ids.shape[0] * ids.shape[1]
    flat = (ids.reshape(rows, 1) == jnp.arange(experts, dtype=jnp.int32)[None, :]).astype(jnp.int32)
    earlier = jnp.cumsum(flat, axis=0) - flat
    position = jnp.sum(earlier * flat, axis=1).reshape(ids.shape)
    return ids * capacity + position


def general(out_grad, expert_ids, gate_weight, saved_hidden, saved_output):
    tokens_here, width = out_grad.shape
    experts = lax.axis_size("expert")
    capacity = saved_hidden.shape[3]
    hidden_width = saved_hidden.shape[4]
    sources = saved_hidden.shape[2]
    slot = slot_numbers(expert_ids, experts, capacity)
    table = slot[:, :, None] == jnp.arange(experts * capacity, dtype=jnp.int32)[None, None, :]
    occupancy = jnp.sum(table, axis=1).astype(jnp.bfloat16)
    sent = lax.dot_general(
        occupancy, out_grad, (((0,), (0,)), ((), ())), preferred_element_type=jnp.float32
    )
    sent = sent.astype(jnp.bfloat16).reshape(experts, capacity, width)
    gate_slots = jnp.sum(jnp.where(table, gate_weight[:, :, None], jnp.float32(0.0)), axis=(0, 1))
    gate_slots = gate_slots.reshape(experts, capacity)
    arrived, arrived_gate = (
        lax.all_to_all(sent, "expert", split_axis=0, concat_axis=0, tiled=True),
        lax.all_to_all(
            gate_slots.astype(jnp.bfloat16), "expert", split_axis=0, concat_axis=0, tiled=True
        ).astype(gate_slots.dtype),
    )
    scaled = (
        (arrived_gate[:, :, None] * arrived).astype(jnp.bfloat16).reshape(sources * capacity, width)
    )
    hidden = saved_hidden.reshape(sources * capacity, hidden_width)
    own_rows = hidden_width // lax.axis_size("dp")
    down_grad = lax.psum_scatter(
        lax.dot_general(
            hidden, scaled, (((0,), (0,)), ((), ())), preferred_element_type=jnp.float32
        ).astype(jnp.bfloat16),
        "dp",
        scatter_dimension=0,
        tiled=True,
    ).astype(jnp.float32)
    down_grad = down_grad.astype(jnp.bfloat16).reshape(1, own_rows, width)
    outputs = saved_output.reshape(sources, capacity, width)
    returned = lax.all_to_all(outputs, "expert", split_axis=0, concat_axis=0, tiled=True)
    picked = returned.reshape(experts * capacity, width)[slot.reshape(-1)]
    picked = picked.reshape(tokens_here, expert_ids.shape[1], width)
    route_grad = jnp.einsum("tkd,td->tk", picked, out_grad, preferred_element_type=jnp.float32)
    return (down_grad, route_grad)


def pack_kernel(grad_ref, ids_ref, gate_ref, out_ref):
    tokens, width = grad_ref.shape
    full, rest = width // LANES, width % LANES
    for j in range(full):
        out_ref[j * tokens:(j + 1) * tokens, :] = grad_ref[:, j * LANES:(j + 1) * LANES]
    tail = grad_ref[:, full * LANES:].astype(jnp.float32)
    out_ref[full * tokens:full * tokens + rest, :] = jnp.concatenate(
        [tail[a * rest:(a + 1) * rest] for a in range(tokens // rest)], axis=1
    ).astype(jnp.bfloat16)
    lane = lax.broadcasted_iota(jnp.int32, (tokens, LANES), 1)
    ids, gate = ids_ref[...], gate_ref[...]
    dense = jnp.zeros((tokens, LANES), jnp.float32)
    for k in range(ids.shape[1]):
        dense = dense + jnp.where(lane == ids[:, k:k + 1], gate[:, k:k + 1], 0.0)
    dense = dense.T[:META // 2]
    high = dense.astype(jnp.bfloat16).astype(jnp.float32)
    out_ref[width:, :] = jnp.concatenate([high, dense - high], axis=0).astype(jnp.bfloat16)


def hidden_kernel(info_ref, hidden_ref, *rest):
    outs, scratch = rest[:-1], rest[-1]
    planes = len(outs)
    rows = outs[0].shape[0]
    for q in range(planes):
        scratch[q] = hidden_ref[:, q * rows:(q + 1) * rows].T
    for o in range(planes):
        outs[o][...] = scratch[info_ref[1] ^ o]


def block_tables(info_ref, mine, other):
    me = info_ref[0]
    width = mine[0].shape[0] - META
    rows = lax.broadcasted_iota(jnp.int32, (META, LANES), 0)
    picked = jnp.logical_or(rows == me, rows == me + META // 2)
    gates = jnp.concatenate(
        [
            jnp.sum(jnp.where(picked, ref[width:, :].astype(jnp.float32), 0.0), axis=0, keepdims=True)
            for ref in mine + other
        ],
        axis=0,
    )
    routed = gates > 0.0
    before = lax.broadcasted_iota(jnp.int32, (LANES, LANES), 0) < lax.broadcasted_iota(jnp.int32, (LANES, LANES), 1)
    earlier = jnp.dot(
        routed.astype(jnp.bfloat16), before.astype(jnp.bfloat16), preferred_element_type=jnp.float32
    ).astype(jnp.int32)
    core = me & 1
    half = LANES // 2
    number = len(mine)
    first = lax.broadcasted_iota(jnp.int32, gates.shape, 0) < number
    side = jnp.where(first, core, 1 - core)
    return gates, jnp.where(routed, earlier + side * half, -1)


def columns(refs, start, stop):
    tokens = LANES
    parts = []
    for ref in refs:
        width = ref.shape[0] - META
        full, rest = width // LANES, width % LANES
        pieces = []
        for j in range(start // LANES, -(-stop // LANES)):
            if j < full:
                pieces.append(ref[j * tokens:(j + 1) * tokens, :])
            else:
                packed = ref[full * tokens:width, :]
                pieces.append(
                    jnp.concatenate([packed[:, a * rest:(a + 1) * rest] for a in range(tokens // rest)], axis=0)
                )
        parts.append(pieces[0] if len(pieces) == 1 else jnp.concatenate(pieces, axis=1))
    return jnp.concatenate(parts, axis=0)


def pair_onehot(position, n, number):
    pair = jnp.concatenate([position[n:n + 1], position[number + n:number + n + 1]], axis=1)
    return lax.broadcasted_iota(jnp.int32, (LANES, 2 * LANES), 0) == pair


def gather_hidden(info_ref, hidden_of, gates, position, number):
    out = []
    for n in range(number):
        start = pl.multiple_of(((info_ref[0] >> 1) ^ n) * LANES, LANES)
        gate = jnp.concatenate([gates[n:n + 1], gates[number + n:number + n + 1]], axis=1)
        placed = jnp.dot(
            hidden_of(start),
            pair_onehot(position, n, number).astype(jnp.bfloat16),
            preferred_element_type=jnp.float32,
        )
        out.append((placed * gate).astype(jnp.bfloat16))
    return jnp.concatenate(out, axis=1)


def interleave(mine, other):
    return [ref for pair in zip(mine, other) for ref in pair]


def column_chunks(width):
    step = 2 * LANES
    return [(a, min(a + step, width)) for a in range(0, width, step)]


def accumulate(hidden, mine, other, acc_ref, out_ref):
    refs = interleave(mine, other)
    width = mine[0].shape[0] - META
    for start, stop in column_chunks(width):
        total = jnp.dot(hidden, columns(refs, start, stop), preferred_element_type=jnp.float32)
        if acc_ref is not None:
            total = total + acc_ref[:, start:stop]
        out_ref[:, start:stop] = total.astype(out_ref.dtype)


def own_kernel(info_ref, hidden_ref, saved_ref, *refs):
    blocks, (acc_ref, score_ref) = refs[:-2], refs[-2:]
    number = len(blocks) // 2
    mine, other = list(blocks[:number]), list(blocks[number:])
    gates, position = block_tables(info_ref, mine, other)
    hidden = gather_hidden(info_ref, lambda s: hidden_ref[:, pl.ds(s, LANES)], gates, position, number)
    accumulate(hidden, mine, other, None, acc_ref)
    width = mine[0].shape[0] - META
    first, second = [], []
    for n in range(number):
        start = pl.multiple_of(((info_ref[0] >> 1) ^ n) * LANES, LANES)
        total = jnp.zeros((LANES, 2 * LANES), jnp.float32)
        for a, b in column_chunks(width):
            total = total + lax.dot_general(
                saved_ref[pl.ds(start, LANES), a:b],
                columns([mine[n], other[n]], a, b),
                (((1,), (1,)), ((), ())),
                preferred_element_type=jnp.float32,
            )
        row = jnp.sum(jnp.where(pair_onehot(position, n, number), total, 0.0), axis=0, keepdims=True)
        first.append(row[:, :LANES])
        second.append(row[:, LANES:])
    score_ref[...] = jnp.concatenate(first + second, axis=0)


def next_kernel(info_ref, near_ref, far_ref, acc_ref, *refs):
    blocks, out_ref = refs[:-1], refs[-1]
    number = len(blocks) // 2
    mine, other = list(blocks[:number]), list(blocks[number:])
    gates, position = block_tables(info_ref, mine, other)

    def hidden_of(start):
        if far_ref is near_ref:
            return near_ref[:, pl.ds(start, LANES)]
        return jnp.where(info_ref[2] != 0, far_ref[:, pl.ds(start, LANES)], near_ref[:, pl.ds(start, LANES)])

    hidden = gather_hidden(info_ref, hidden_of, gates, position, number)
    accumulate(hidden, mine, other, acc_ref, out_ref)


def one_hidden_kernel(info_ref, near_ref, acc_ref, *refs):
    next_kernel(info_ref, near_ref, near_ref, acc_ref, *refs)


def call(kernel, outs, args, scratch=(), flops=0):
    smem, vmem = pl.BlockSpec(memory_space=pltpu.SMEM), pl.BlockSpec(memory_space=pltpu.VMEM)
    moved = sum(a.size * a.dtype.itemsize for a in (*args, *outs))
    return pl.pallas_call(
        kernel,
        out_shape=outs,
        in_specs=[smem if a.ndim == 1 else vmem for a in args],
        out_specs=[vmem] * len(outs),
        scratch_shapes=list(scratch),
        compiler_params=pltpu.CompilerParams(vmem_limit_bytes=48 * 1024 * 1024),
        cost_estimate=pl.CostEstimate(flops=flops, bytes_accessed=moved, transcendentals=0),
    )(*args)


def planes4(out_grad, expert_ids, gate_weight, saved_hidden, saved_output):
    tokens, width = out_grad.shape
    hidden_width = saved_hidden.shape[4]
    slots = saved_hidden.shape[2] * saved_hidden.shape[3]
    planes = lax.axis_size("dp")
    rows = hidden_width // planes
    me, plane = lax.axis_index("expert"), lax.axis_index("dp")
    middle = jnp.logical_or(plane == 1, plane == 2)
    bf16 = jnp.bfloat16

    def along(name, bit):
        return lambda x: lax.ppermute(x, name, [(i, i ^ bit) for i in range(lax.axis_size(name))])

    core, px, py = along("expert", 1), along("expert", 2), along("expert", 4)
    inner = lambda x: lax.ppermute(x, "dp", [(1, 2), (2, 1)])
    outward = lambda x: lax.ppermute(x, "dp", [(1, 0), (2, 3)])
    info = jnp.stack([me, plane, middle.astype(jnp.int32)]).astype(jnp.int32)
    info_flip = jnp.stack([me, plane, 1 - middle.astype(jnp.int32)]).astype(jnp.int32)

    packed = jax.ShapeDtypeStruct((width + META, LANES), bf16)
    (own,) = call(pack_kernel, [packed], (out_grad, expert_ids, gate_weight))
    near = along("dp", 1)(own)
    across = inner(own)
    hidden = call(
        hidden_kernel,
        [jax.ShapeDtypeStruct((rows, slots), bf16)] * planes,
        (info, saved_hidden.reshape(slots, hidden_width)),
        scratch=[pltpu.VMEM((planes, rows, slots), bf16)],
    )
    second_in = inner(near)
    second_out = outward(across)
    third_out = outward(second_in)
    sets = [own, near, jnp.where(middle, across, second_out), jnp.where(middle, second_in, third_out)]
    arrived = [hidden[0]] + [along("dp", o)(hidden[o]) for o in range(1, planes)]

    blocks = []
    for number, block in enumerate(sets):
        bx, by = px(block), py(block)
        diagonal = px(by) if number % 2 == 0 else py(bx)
        mine = [block, bx, by, diagonal]
        blocks.append(mine + [core(b) for b in mine])

    flops = 2 * rows * width * 8 * tokens
    acc = jax.ShapeDtypeStruct((rows, width), jnp.float32)
    total, score = call(
        own_kernel,
        [acc, jax.ShapeDtypeStruct((8, LANES), jnp.float32)],
        (info, arrived[0], saved_output.reshape(slots, width), *blocks[0]),
        flops=flops,
    )
    (total,) = call(one_hidden_kernel, [acc], (info, arrived[1], total, *blocks[1]), flops=flops)
    (total,) = call(next_kernel, [acc], (info, arrived[2], arrived[3], total, *blocks[2]), flops=flops)
    (down_grad,) = call(
        next_kernel,
        [jax.ShapeDtypeStruct((rows, width), bf16)],
        (info_flip, arrived[2], arrived[3], total, *blocks[3]),
        flops=flops,
    )

    scores = score[None]
    scores = jnp.concatenate([scores, px(scores)], axis=0)
    scores = jnp.concatenate([scores, py(scores)], axis=0)
    scores = jnp.concatenate([scores, core(scores)], axis=0)
    offsets = [0, 2, 4, 6, 1, 3, 5, 7]
    back = jnp.stack([scores[n, n] for n in range(8)])
    wanted = (expert_ids ^ me)[:, :, None] == jnp.array(offsets, jnp.int32)[None, None, :]
    route_grad = jnp.sum(jnp.where(wanted, back.T[:, None, :], 0.0), axis=-1)
    return (down_grad.reshape(1, rows, width), route_grad)


def fits(mesh, out_grad, expert_ids, gate_weight, saved_hidden, saved_output):
    planes, experts = mesh.shape["dp"], mesh.shape["expert"]
    tokens, width = out_grad.shape[0] // (planes * experts), out_grad.shape[1]
    rest = width % LANES
    return (
        planes == 4
        and experts == 8
        and tokens == LANES
        and 2 * saved_hidden.shape[3] == LANES
        and saved_hidden.shape[4] % (8 * planes) == 0
        and rest > 0
        and rest % 8 == 0
        and LANES % rest == 0
    )


def solution(mesh):
    placed = (
        P(("dp", "expert"), None),
        P(("dp", "expert"), None),
        P(("dp", "expert"), None),
        P("dp", "expert", None, None, None),
        P("dp", "expert", None, None, None),
    )

    def run(*arrays):
        return jax.shard_map(
            planes4 if fits(mesh, *arrays) else general,
            mesh=mesh,
            in_specs=placed,
            out_specs=(P("expert", "dp", None), P(("dp", "expert"), None)),
            check_vma=False,
        )(*arrays)

    return run
```

```python
import functools

import jax
import jax.numpy as jnp
from jax import lax
from jax.experimental import pallas as pl
from jax.experimental.pallas import tpu as pltpu
from jax.sharding import PartitionSpec as P

LANES = 128
META = 16


def slot_numbers(ids, experts, capacity):
    rows = ids.shape[0] * ids.shape[1]
    flat = (ids.reshape(rows, 1) == jnp.arange(experts, dtype=jnp.int32)[None, :]).astype(jnp.int32)
    earlier = jnp.cumsum(flat, axis=0) - flat
    position = jnp.sum(earlier * flat, axis=1).reshape(ids.shape)
    return ids * capacity + position


def general(out_grad, expert_ids, gate_weight, saved_hidden, saved_output):
    tokens_here, width = out_grad.shape
    experts = lax.axis_size("expert")
    capacity = saved_hidden.shape[3]
    hidden_width = saved_hidden.shape[4]
    sources = saved_hidden.shape[2]
    slot = slot_numbers(expert_ids, experts, capacity)
    table = slot[:, :, None] == jnp.arange(experts * capacity, dtype=jnp.int32)[None, None, :]
    occupancy = jnp.sum(table, axis=1).astype(jnp.bfloat16)
    sent = lax.dot_general(
        occupancy, out_grad, (((0,), (0,)), ((), ())), preferred_element_type=jnp.float32
    )
    sent = sent.astype(jnp.bfloat16).reshape(experts, capacity, width)
    gate_slots = jnp.sum(jnp.where(table, gate_weight[:, :, None], jnp.float32(0.0)), axis=(0, 1))
    gate_slots = gate_slots.reshape(experts, capacity)
    arrived, arrived_gate = (
        lax.all_to_all(sent, "expert", split_axis=0, concat_axis=0, tiled=True),
        lax.all_to_all(
            gate_slots.astype(jnp.bfloat16), "expert", split_axis=0, concat_axis=0, tiled=True
        ).astype(gate_slots.dtype),
    )
    scaled = (
        (arrived_gate[:, :, None] * arrived).astype(jnp.bfloat16).reshape(sources * capacity, width)
    )
    hidden = saved_hidden.reshape(sources * capacity, hidden_width)
    own_rows = hidden_width // lax.axis_size("dp")
    down_grad = lax.psum_scatter(
        lax.dot_general(
            hidden, scaled, (((0,), (0,)), ((), ())), preferred_element_type=jnp.float32
        ).astype(jnp.bfloat16),
        "dp",
        scatter_dimension=0,
        tiled=True,
    ).astype(jnp.float32)
    down_grad = down_grad.astype(jnp.bfloat16).reshape(1, own_rows, width)
    outputs = saved_output.reshape(sources, capacity, width)
    returned = lax.all_to_all(outputs, "expert", split_axis=0, concat_axis=0, tiled=True)
    picked = returned.reshape(experts * capacity, width)[slot.reshape(-1)]
    picked = picked.reshape(tokens_here, expert_ids.shape[1], width)
    route_grad = jnp.einsum("tkd,td->tk", picked, out_grad, preferred_element_type=jnp.float32)
    return (down_grad, route_grad)


def pack_kernel(grad_ref, ids_ref, gate_ref, out_ref):
    width, tokens = grad_ref.shape
    out_ref[:width, :] = grad_ref[...]
    expert = lax.broadcasted_iota(jnp.int32, (META // 2, tokens), 0)
    dense = jnp.zeros((META // 2, tokens), jnp.float32)
    for k in range(ids_ref.shape[0]):
        dense = dense + jnp.where(expert == ids_ref[k:k + 1, :], gate_ref[k:k + 1, :], 0.0)
    high = dense.astype(jnp.bfloat16).astype(jnp.float32)
    out_ref[width:, :] = jnp.concatenate([high, dense - high], axis=0).astype(jnp.bfloat16)


def rows_of_core(ref, core, cols):
    return jnp.concatenate([ref[c, core, :, cols] for c in range(ref.shape[0])], axis=0)


def turn_kernel(info_ref, hidden_ref, keep_ref, leave_ref):
    core = info_ref[0] & 1
    width = hidden_ref.shape[3]
    for a in range(0, width, LANES):
        cols = slice(a, min(a + LANES, width))
        keep_ref[cols, :] = rows_of_core(hidden_ref, core, cols).T
        leave_ref[cols, :] = rows_of_core(hidden_ref, 1 - core, cols).T


def quarter_kernel(info_ref, keep_ref, got_ref, *rest):
    outs, scratch = rest[:-1], rest[-1]
    planes, rows, half = len(outs), outs[0].shape[0], keep_ref.shape[1]
    for q in range(planes):
        scratch[q, :, :half] = keep_ref[q * rows:(q + 1) * rows, :]
        scratch[q, :, half:] = got_ref[q * rows:(q + 1) * rows, :]
    for o in range(planes):
        outs[o][...] = scratch[info_ref[1] ^ o]


def saved_kernel(info_ref, saved_ref, out_ref):
    theirs = 1 - (info_ref[0] & 1)
    rows, width = saved_ref.shape[0] * saved_ref.shape[2], saved_ref.shape[3]
    full, rest = width // LANES, width % LANES
    for j in range(full):
        out_ref[j * rows:(j + 1) * rows, :] = rows_of_core(saved_ref, theirs, slice(j * LANES, (j + 1) * LANES))
    tail = rows_of_core(saved_ref, theirs, slice(full * LANES, width)).astype(jnp.float32)
    step = rows * rest // LANES
    out_ref[full * rows:, :] = jnp.concatenate(
        [tail[a * step:(a + 1) * step] for a in range(LANES // rest)], axis=1
    ).astype(jnp.bfloat16)


def block_tables(info_ref, blocks):
    me = info_ref[0]
    core, chip = me & 1, me >> 1
    offsets = [0, 1 + core, 2 - core, 3]
    width = blocks[0].shape[0] - META
    rows = lax.broadcasted_iota(jnp.int32, (META, LANES), 0)
    metas = [ref[width:, :].astype(jnp.float32) for ref in blocks]
    gates = []
    for expert in (me, me ^ 1):
        picked = jnp.logical_or(rows == expert, rows == expert + META // 2)
        gates += [jnp.sum(jnp.where(picked, meta, 0.0), axis=0, keepdims=True) for meta in metas]
    gates = jnp.concatenate(gates, axis=0)
    routed = gates > 0.0
    before = lax.broadcasted_iota(jnp.int32, (LANES, LANES), 0) < lax.broadcasted_iota(jnp.int32, (LANES, LANES), 1)
    earlier = jnp.dot(
        routed.astype(jnp.bfloat16), before.astype(jnp.bfloat16), preferred_element_type=jnp.float32
    ).astype(jnp.int32)
    position = jnp.where(routed, earlier, -LANES * LANES)
    number = len(blocks)
    out = []
    for w in range(2):
        gate = jnp.concatenate([gates[w * number + n:w * number + n + 1] for n in range(number)], axis=1)
        place = jnp.concatenate(
            [position[w * number + n:w * number + n + 1] + (chip ^ offsets[n]) * (LANES // 2) for n in range(number)],
            axis=1,
        )
        out.append((gate, place))
    return out


def chosen(place, slots):
    return lax.broadcasted_iota(jnp.int32, (slots, place.shape[1]), 0) == place


def gather_hidden(hidden, table):
    gate, place = table
    placed = jnp.dot(
        hidden, chosen(place, hidden.shape[1]).astype(jnp.bfloat16), preferred_element_type=jnp.float32
    )
    return (placed * gate).astype(jnp.bfloat16)


def chunks(width, step=2 * LANES):
    return [(a, min(a + step, width)) for a in range(0, width, step)]


def tokens_of(blocks, a, b):
    return jnp.concatenate([ref[a:b, :] for ref in blocks], axis=1)


def accumulate(hidden, blocks, acc_refs, out_refs):
    width = blocks[0].shape[0] - META
    rows = out_refs[0].shape[0]
    for a, b in chunks(width):
        total = lax.dot_general(
            hidden, tokens_of(blocks, a, b), (((1,), (1,)), ((), ())), preferred_element_type=jnp.float32
        )
        for w, out_ref in enumerate(out_refs):
            value = total[w * rows:(w + 1) * rows]
            if acc_refs:
                value = value + acc_refs[w][:, a:b]
            out_ref[:, a:b] = value.astype(out_ref.dtype)


def hidden_part(info_ref, hidden_refs, w):
    half = hidden_refs[0].shape[1] // 2
    picked = [ref[:, w * half:(w + 1) * half] for ref in hidden_refs]
    if len(picked) == 1:
        return picked[0]
    return jnp.where(info_ref[2] != 0, picked[1], picked[0])


def sum_kernel(hiddens, experts, started, info_ref, *refs):
    hidden_refs, refs = refs[:hiddens], refs[hiddens:]
    number = len(experts)
    outs, refs = refs[-number:], refs[:-number]
    accs, blocks = (refs[:number], list(refs[number:])) if started else ((), list(refs))
    tables = block_tables(info_ref, blocks)
    hidden = [gather_hidden(hidden_part(info_ref, hidden_refs, w), tables[w]) for w in experts]
    accumulate(hidden[0] if number == 1 else jnp.concatenate(hidden, axis=0), blocks, accs, outs)


def score_kernel(info_ref, saved_ref, got_ref, *refs):
    blocks, score_ref = list(refs[:-1]), refs[-1]
    tables = block_tables(info_ref, blocks)
    core = info_ref[0] & 1
    rows, width = saved_ref.shape[0] * saved_ref.shape[2], saved_ref.shape[3]
    full, rest = width // LANES, width % LANES
    total = jnp.zeros((2 * rows, len(blocks) * LANES), jnp.float32)
    for a, b in chunks(width):
        pieces = []
        for j in range(a // LANES, -(-b // LANES)):
            if j < full:
                pieces.append(got_ref[j * rows:(j + 1) * rows, :])
            else:
                tail = got_ref[full * rows:, :]
                pieces.append(
                    jnp.concatenate([tail[:, n * rest:(n + 1) * rest] for n in range(LANES // rest)], axis=0)
                )
        theirs = pieces[0] if len(pieces) == 1 else jnp.concatenate(pieces, axis=1)
        saved = jnp.concatenate([rows_of_core(saved_ref, core, slice(a, b)), theirs], axis=0)
        total = total + jnp.dot(saved, tokens_of(blocks, a, b), preferred_element_type=jnp.float32)
    scores = []
    for w in range(2):
        row = jnp.sum(
            jnp.where(chosen(tables[w][1], rows), total[w * rows:(w + 1) * rows], 0.0), axis=0, keepdims=True
        )
        scores += [row[:, n * LANES:(n + 1) * LANES] for n in range(len(blocks))]
    score_ref[...] = jnp.concatenate(scores, axis=0)


def add_kernel(a_ref, b_ref, out_ref):
    out_ref[...] = (a_ref[...] + b_ref[...].astype(jnp.float32)).astype(out_ref.dtype)


def call(kernel, outs, args, scratch=(), flops=0, limit=16):
    smem, vmem = pl.BlockSpec(memory_space=pltpu.SMEM), pl.BlockSpec(memory_space=pltpu.VMEM)
    moved = sum(a.size * a.dtype.itemsize for a in (*args, *outs))
    return pl.pallas_call(
        kernel,
        out_shape=outs,
        in_specs=[smem if a.ndim == 1 else vmem for a in args],
        out_specs=[vmem] * len(outs),
        scratch_shapes=list(scratch),
        compiler_params=pltpu.CompilerParams(vmem_limit_bytes=limit * 1024 * 1024),
        cost_estimate=pl.CostEstimate(flops=flops, bytes_accessed=moved, transcendentals=0),
    )(*args)


def after(value, *earlier):
    return lax.optimization_barrier((value, *earlier))[0]


def planes4(out_grad, expert_ids, gate_weight, saved_hidden, saved_output):
    tokens, width = out_grad.shape
    hidden_width = saved_hidden.shape[4]
    sources, capacity = saved_hidden.shape[2:4]
    slots = sources * capacity
    planes = lax.axis_size("dp")
    rows = hidden_width // planes
    me, plane = lax.axis_index("expert"), lax.axis_index("dp")
    middle = jnp.logical_or(plane == 1, plane == 2)
    bf16 = jnp.bfloat16

    def permute(name, target):
        return lambda x: lax.ppermute(x, name, [(i, target(i)) for i in range(lax.axis_size(name))])

    core = permute("expert", lambda i: i ^ 1)
    first = permute("expert", lambda i: i ^ (4 if i & 1 else 2))
    second = permute("expert", lambda i: i ^ (2 if i & 1 else 4))
    diagonal = permute("expert", lambda i: i ^ 6)
    near_plane, far2, far3 = (permute("dp", lambda i, o=o: i ^ o) for o in (1, 2, 3))
    inner = lambda x: lax.ppermute(x, "dp", [(1, 2), (2, 1)])
    outward = lambda x: lax.ppermute(x, "dp", [(1, 0), (2, 3)])
    info = jnp.stack([me, plane, middle.astype(jnp.int32)]).astype(jnp.int32)
    info_flip = jnp.stack([me, plane, 1 - middle.astype(jnp.int32)]).astype(jnp.int32)
    hidden4 = saved_hidden.reshape(sources // 2, 2, capacity, hidden_width)
    saved4 = saved_output.reshape(sources // 2, 2, capacity, width)

    def shaped(*shape, dtype=bf16):
        return jax.ShapeDtypeStruct(shape, dtype)

    acc = shaped(rows, width, dtype=jnp.float32)
    flops = 4 * rows * width * 4 * tokens

    (own,) = call(pack_kernel, [shaped(width + META, tokens)], (out_grad.T, expert_ids.T, gate_weight.T))
    near, across = near_plane(own), inner(own)
    a0, b0 = first(own), second(own)
    kept, leaving = call(turn_kernel, [shaped(hidden_width, slots // 2)] * 2, (info, hidden4))
    hidden = call(
        quarter_kernel,
        [shaped(rows, slots)] * planes,
        (info, kept, core(leaving)),
        scratch=[pltpu.VMEM((planes, rows, slots), bf16)],
    )
    (saved_leaving,) = call(saved_kernel, [shaped(width * slots // 2 // LANES, LANES)], (info, saved4))
    saved_got = core(saved_leaving)
    second_in, second_out = inner(near), outward(across)
    d0 = second(a0)
    a1, b1 = first(near), second(near)
    totals = call(
        functools.partial(sum_kernel, 1, (0, 1), False), [acc, acc], (info, hidden[0], own, a0, b0, d0), flops=flops
    )
    (score,) = call(
        score_kernel, [shaped(8, LANES, dtype=jnp.float32)], (info, saved4, saved_got, own, a0, b0, d0),
        flops=4 * slots * width * tokens,
    )
    third_out = outward(second_in)
    h3 = far3(after(hidden[3], second_in, second_out))
    block2 = jnp.where(middle, across, second_out)
    d1 = second(a1)
    a2, b2 = first(after(block2, a1)), second(after(block2, b1))
    block3 = jnp.where(middle, second_in, third_out)
    h2 = far2(after(hidden[2], h3, third_out))
    h1 = near_plane(after(hidden[1], h3, third_out))
    d2 = second(a2)
    a3, b3 = first(after(block3, a2)), second(after(block3, b2))
    d3 = second(a3)

    ra, rb, rd = first(score), second(score), diagonal(score)

    totals = call(
        functools.partial(sum_kernel, 1, (0, 1), True), [acc, acc], (info, h1, *totals, near, a1, b1, d1), flops=flops
    )
    own_total, other_total = call(
        functools.partial(sum_kernel, 2, (0, 1), True), [acc, acc],
        (info, h2, h3, *totals, block2, a2, b2, d2), flops=flops,
    )
    (leaving_part,) = call(
        functools.partial(sum_kernel, 2, (1,), True), [shaped(rows, width)],
        (info_flip, h2, h3, other_total, block3, a3, b3, d3), flops=flops // 2,
    )
    got_part = core(leaving_part)
    (own_total,) = call(
        functools.partial(sum_kernel, 2, (0,), True), [acc],
        (info_flip, h2, h3, own_total, block3, a3, b3, d3), flops=flops // 2,
    )
    (down_grad,) = call(add_kernel, [shaped(rows, width)], (own_total, got_part))

    odd = me & 1
    offsets = jnp.stack([0 * odd, 2 + 2 * odd, 4 - 2 * odd, 6 + 0 * odd])
    offsets = jnp.concatenate([offsets, offsets ^ 1])
    back = jnp.stack([r[4 * w + n] for w in range(2) for n, r in enumerate((score, ra, rb, rd))])
    wanted = (expert_ids.T ^ me)[:, None, :] == offsets[None, :, None]
    route_grad = jnp.sum(jnp.where(wanted, back[None], 0.0), axis=1).T
    return (down_grad.reshape(1, rows, width), route_grad)


def fits(mesh, out_grad, expert_ids, gate_weight, saved_hidden, saved_output):
    planes, experts = mesh.shape["dp"], mesh.shape["expert"]
    tokens, width = out_grad.shape[0] // (planes * experts), out_grad.shape[1]
    rest = width % LANES
    return (
        planes == 4
        and experts == 8
        and tokens == LANES
        and 2 * saved_hidden.shape[3] == LANES
        and saved_hidden.shape[4] % (8 * planes) == 0
        and rest > 0
        and rest % 8 == 0
        and LANES % rest == 0
    )


def solution(mesh):
    placed = (
        P(("dp", "expert"), None),
        P(("dp", "expert"), None),
        P(("dp", "expert"), None),
        P("dp", "expert", None, None, None),
        P("dp", "expert", None, None, None),
    )

    def run(*arrays):
        return jax.shard_map(
            planes4 if fits(mesh, *arrays) else general,
            mesh=mesh,
            in_specs=placed,
            out_specs=(P("expert", "dp", None), P(("dp", "expert"), None)),
            check_vma=False,
        )(*arrays)

    return run
```

```python
import functools

import jax
import jax.numpy as jnp
from jax import lax
from jax.experimental import pallas as pl
from jax.experimental.pallas import tpu as pltpu
from jax.sharding import PartitionSpec as P

LANES = 128
META = 16


def slot_numbers(ids, experts, capacity):
    rows = ids.shape[0] * ids.shape[1]
    flat = (ids.reshape(rows, 1) == jnp.arange(experts, dtype=jnp.int32)[None, :]).astype(jnp.int32)
    earlier = jnp.cumsum(flat, axis=0) - flat
    position = jnp.sum(earlier * flat, axis=1).reshape(ids.shape)
    return ids * capacity + position


def general(out_grad, expert_ids, gate_weight, saved_hidden, saved_output):
    tokens_here, width = out_grad.shape
    experts = lax.axis_size("expert")
    capacity = saved_hidden.shape[3]
    hidden_width = saved_hidden.shape[4]
    sources = saved_hidden.shape[2]
    slot = slot_numbers(expert_ids, experts, capacity)
    table = slot[:, :, None] == jnp.arange(experts * capacity, dtype=jnp.int32)[None, None, :]
    occupancy = jnp.sum(table, axis=1).astype(jnp.bfloat16)
    sent = lax.dot_general(
        occupancy, out_grad, (((0,), (0,)), ((), ())), preferred_element_type=jnp.float32
    )
    sent = sent.astype(jnp.bfloat16).reshape(experts, capacity, width)
    gate_slots = jnp.sum(jnp.where(table, gate_weight[:, :, None], jnp.float32(0.0)), axis=(0, 1))
    gate_slots = gate_slots.reshape(experts, capacity)
    arrived, arrived_gate = (
        lax.all_to_all(sent, "expert", split_axis=0, concat_axis=0, tiled=True),
        lax.all_to_all(
            gate_slots.astype(jnp.bfloat16), "expert", split_axis=0, concat_axis=0, tiled=True
        ).astype(gate_slots.dtype),
    )
    scaled = (
        (arrived_gate[:, :, None] * arrived).astype(jnp.bfloat16).reshape(sources * capacity, width)
    )
    hidden = saved_hidden.reshape(sources * capacity, hidden_width)
    own_rows = hidden_width // lax.axis_size("dp")
    down_grad = lax.psum_scatter(
        lax.dot_general(
            hidden, scaled, (((0,), (0,)), ((), ())), preferred_element_type=jnp.float32
        ).astype(jnp.bfloat16),
        "dp",
        scatter_dimension=0,
        tiled=True,
    ).astype(jnp.float32)
    down_grad = down_grad.astype(jnp.bfloat16).reshape(1, own_rows, width)
    outputs = saved_output.reshape(sources, capacity, width)
    returned = lax.all_to_all(outputs, "expert", split_axis=0, concat_axis=0, tiled=True)
    picked = returned.reshape(experts * capacity, width)[slot.reshape(-1)]
    picked = picked.reshape(tokens_here, expert_ids.shape[1], width)
    route_grad = jnp.einsum("tkd,td->tk", picked, out_grad, preferred_element_type=jnp.float32)
    return (down_grad, route_grad)


def pack_kernel(grad_ref, ids_ref, gate_ref, out_ref, ids, gate, sems):
    width, tokens = grad_ref.shape[2:]
    copies = [
        pltpu.make_async_copy(ids_ref.at[0, 0], ids, sems.at[0]),
        pltpu.make_async_copy(gate_ref.at[0, 0], gate, sems.at[1]),
        pltpu.make_async_copy(grad_ref.at[0, 0], out_ref.at[:width], sems.at[2]),
    ]
    for copy in copies:
        copy.start()
    copies[0].wait()
    copies[1].wait()
    expert = lax.broadcasted_iota(jnp.int32, (META // 2, tokens), 0)
    dense = jnp.zeros((META // 2, tokens), jnp.float32)
    for k in range(ids.shape[0]):
        dense = dense + jnp.where(expert == ids[k:k + 1, :], gate[k:k + 1, :], 0.0)
    high = dense.astype(jnp.bfloat16).astype(jnp.float32)
    out_ref[width:, :] = jnp.concatenate([high, dense - high], axis=0).astype(jnp.bfloat16)
    copies[2].wait()


def fetch(source, target, sems, cores):
    copies = [
        pltpu.make_async_copy(source.at[c, core], target.at[c, n], sems.at[c, n])
        for c in range(source.shape[0])
        for n, core in enumerate(cores)
    ]
    for copy in copies:
        copy.start()
    for copy in copies:
        copy.wait()


def stacked(ref, n, cols):
    return jnp.concatenate([ref[c, n, :, cols] for c in range(ref.shape[0])], axis=0)


def turn_kernel(info_ref, hidden_ref, keep_ref, leave_ref, here, sems):
    core = info_ref[0] & 1
    fetch(hidden_ref, here, sems, (core, 1 - core))
    width = here.shape[3]
    for a in range(0, width, LANES):
        cols = slice(a, min(a + LANES, width))
        keep_ref[cols, :] = stacked(here, 0, cols).T
        leave_ref[cols, :] = stacked(here, 1, cols).T


def quarter_kernel(info_ref, keep_ref, got_ref, *rest):
    outs, scratch = rest[:-1], rest[-1]
    planes, rows, half = len(outs), outs[0].shape[0], keep_ref.shape[1]
    for q in range(planes):
        scratch[q, :, :half] = keep_ref[q * rows:(q + 1) * rows, :]
        scratch[q, :, half:] = got_ref[q * rows:(q + 1) * rows, :]
    for o in range(planes):
        outs[o][...] = scratch[info_ref[1] ^ o]


def saved_kernel(info_ref, saved_ref, out_ref, here, sems):
    fetch(saved_ref, here, sems, (1 - (info_ref[0] & 1),))
    rows, width = here.shape[0] * here.shape[2], here.shape[3]
    full, rest = width // LANES, width % LANES
    for j in range(full):
        out_ref[j * rows:(j + 1) * rows, :] = stacked(here, 0, slice(j * LANES, (j + 1) * LANES))
    tail = stacked(here, 0, slice(full * LANES, width)).astype(jnp.float32)
    step = rows * rest // LANES
    out_ref[full * rows:, :] = jnp.concatenate(
        [tail[a * step:(a + 1) * step] for a in range(LANES // rest)], axis=1
    ).astype(jnp.bfloat16)


def choose_kernel(info_ref, inner_ref, outer_ref, *refs):
    out_ref = refs[-1]
    rows = inner_ref.shape[0]
    middle = jnp.logical_or(info_ref[1] == 1, info_ref[1] == 2)

    @pl.when(middle)
    def _():
        out_ref[:rows, :] = inner_ref[...]

    @pl.when(jnp.logical_not(middle))
    def _():
        out_ref[:rows, :] = outer_ref[...]

    if len(refs) > 1:
        score = refs[0][...]
        high = score.astype(jnp.bfloat16).astype(jnp.float32)
        out_ref[rows:, :] = jnp.concatenate([high, score - high], axis=0).astype(jnp.bfloat16)


def join_kernel(a_ref, b_ref, out_ref):
    out_ref[0] = a_ref[...]
    out_ref[1] = b_ref[...]


def block_tables(info_ref, blocks, width):
    me = info_ref[0]
    core, chip = me & 1, me >> 1
    offsets = [0, 1 + core, 2 - core, 3]
    rows = lax.broadcasted_iota(jnp.int32, (META, LANES), 0)
    metas = [ref[width:width + META, :].astype(jnp.float32) for ref in blocks]
    gates = []
    for expert in (me, me ^ 1):
        picked = jnp.logical_or(rows == expert, rows == expert + META // 2)
        gates += [jnp.sum(jnp.where(picked, meta, 0.0), axis=0, keepdims=True) for meta in metas]
    gates = jnp.concatenate(gates, axis=0)
    routed = gates > 0.0
    before = lax.broadcasted_iota(jnp.int32, (LANES, LANES), 0) < lax.broadcasted_iota(jnp.int32, (LANES, LANES), 1)
    earlier = jnp.dot(
        routed.astype(jnp.bfloat16), before.astype(jnp.bfloat16), preferred_element_type=jnp.float32
    ).astype(jnp.int32)
    position = jnp.where(routed, earlier, -LANES * LANES)
    number = len(blocks)
    out = []
    for w in range(2):
        gate = jnp.concatenate([gates[w * number + n:w * number + n + 1] for n in range(number)], axis=1)
        place = jnp.concatenate(
            [position[w * number + n:w * number + n + 1] + (chip ^ offsets[n]) * (LANES // 2) for n in range(number)],
            axis=1,
        )
        out.append((gate, place))
    return out


def chosen(place, slots):
    return lax.broadcasted_iota(jnp.int32, (slots, place.shape[1]), 0) == place


def gather_hidden(hidden, table):
    gate, place = table
    placed = jnp.dot(
        hidden, chosen(place, hidden.shape[1]).astype(jnp.bfloat16), preferred_element_type=jnp.float32
    )
    return (placed * gate).astype(jnp.bfloat16)


def chunks(width, step=2 * LANES):
    return [(a, min(a + step, width)) for a in range(0, width, step)]


def tokens_of(blocks, a, b):
    return jnp.concatenate([ref[a:b, :] for ref in blocks], axis=1)


def accumulate(hidden, blocks, width, acc_refs, out_refs):
    rows = out_refs[0].shape[0]
    for a, b in chunks(width):
        total = lax.dot_general(
            hidden, tokens_of(blocks, a, b), (((1,), (1,)), ((), ())), preferred_element_type=jnp.float32
        )
        for w, out_ref in enumerate(out_refs):
            value = total[w * rows:(w + 1) * rows]
            if acc_refs:
                value = value + acc_refs[w][:, a:b]
            out_ref[:, a:b] = value.astype(out_ref.dtype)


def four(refs):
    own, first, pair = refs
    return [own, first, pair.at[0], pair.at[1]]


def sum_kernel(choices, experts, started, info_ref, *refs):
    hidden_refs, refs = refs[:choices], refs[choices:]
    number = len(experts)
    outs, refs = refs[-number:], refs[:-number]
    accs, refs = (refs[:number], refs[number:]) if started else ((), refs)
    blocks, width = four(refs), outs[0].shape[1]
    tables = block_tables(info_ref, blocks, width)
    half = hidden_refs[0].shape[1] // 2
    middle = jnp.logical_or(info_ref[1] == 1, info_ref[1] == 2)
    hidden = []
    for w in experts:
        parts = [ref[:, w * half:(w + 1) * half] for ref in hidden_refs]
        hidden.append(gather_hidden(parts[0] if choices == 1 else jnp.where(middle, *parts), tables[w]))
    accumulate(hidden[0] if number == 1 else jnp.concatenate(hidden, axis=0), blocks, width, accs, outs)


def score_kernel(info_ref, saved_ref, got_ref, *refs):
    blocks, (score_ref, here, sems) = four(refs[:-3]), refs[-3:]
    fetch(saved_ref, here, sems, (info_ref[0] & 1,))
    rows, width = here.shape[0] * here.shape[2], here.shape[3]
    tables = block_tables(info_ref, blocks, width)
    full, rest = width // LANES, width % LANES
    total = jnp.zeros((2 * rows, len(blocks) * LANES), jnp.float32)
    for a, b in chunks(width):
        pieces = []
        for j in range(a // LANES, -(-b // LANES)):
            if j < full:
                pieces.append(got_ref[j * rows:(j + 1) * rows, :])
            else:
                tail = got_ref[full * rows:, :]
                pieces.append(
                    jnp.concatenate([tail[:, n * rest:(n + 1) * rest] for n in range(LANES // rest)], axis=0)
                )
        theirs = pieces[0] if len(pieces) == 1 else jnp.concatenate(pieces, axis=1)
        saved = jnp.concatenate([stacked(here, 0, slice(a, b)), theirs], axis=0)
        total = total + jnp.dot(saved, tokens_of(blocks, a, b), preferred_element_type=jnp.float32)
    scores = []
    for w in range(2):
        row = jnp.sum(
            jnp.where(chosen(tables[w][1], rows), total[w * rows:(w + 1) * rows], 0.0), axis=0, keepdims=True
        )
        scores += [row[:, n * LANES:(n + 1) * LANES] for n in range(len(blocks))]
    score_ref[...] = jnp.concatenate(scores, axis=0)


def route_kernel(info_ref, ids_ref, score_ref, first_ref, pair_ref, out_ref, ids, sem):
    copy = pltpu.make_async_copy(ids_ref.at[0, 0], ids, sem)
    copy.start()
    half = META // 2
    parts = [score_ref[...]]
    for ref in (first_ref, pair_ref.at[0], pair_ref.at[1]):
        sent = ref[ref.shape[0] - META:, :].astype(jnp.float32)
        parts.append(sent[:half] + sent[half:])
    me = info_ref[0]
    core = me & 1
    offsets = [0, 2 + 2 * core, 4 - 2 * core, 6]
    copy.wait()
    wanted = ids[...] ^ me
    total = jnp.zeros(wanted.shape, jnp.float32)
    for w in range(2):
        for n, part in enumerate(parts):
            total = total + jnp.where(wanted == offsets[n] ^ w, part[4 * w + n:4 * w + n + 1], 0.0)
    out_ref[...] = total


def add_kernel(a_ref, b_ref, out_ref):
    out_ref[...] = (a_ref[...] + b_ref[...].astype(jnp.float32)).astype(out_ref.dtype)


def call(kernel, outs, args, scratch=(), flops=0, limit=8, aliases=None):
    smem, vmem, hbm = (pl.BlockSpec(memory_space=space) for space in (pltpu.SMEM, pltpu.VMEM, pltpu.HBM))
    moved = sum(a.size * a.dtype.itemsize for a in args)
    specs, operands = [], []
    for a in args:
        specs.append(smem if a.ndim == 1 else hbm if a.ndim == 4 else vmem)
        if a.ndim > 1:
            a = pltpu.with_memory_space_constraint(a, pltpu.HBM if a.ndim == 4 else pltpu.VMEM)
        operands.append(a)
    return pl.pallas_call(
        kernel,
        out_shape=outs,
        in_specs=specs,
        out_specs=[vmem] * len(outs),
        scratch_shapes=list(scratch),
        input_output_aliases=aliases or {},
        compiler_params=pltpu.CompilerParams(vmem_limit_bytes=limit * 1024 * 1024),
        cost_estimate=pl.CostEstimate(flops=5 * flops, bytes_accessed=5 * moved, transcendentals=0),
    )(*operands)


def phase(*values):
    return lax.optimization_barrier(values)


def after(value, *earlier):
    return phase(value, *earlier)[0]


def planes4(out_grad, expert_ids, gate_weight, saved_hidden, saved_output):
    tokens, width = out_grad.shape
    hidden_width = saved_hidden.shape[4]
    sources, capacity = saved_hidden.shape[2:4]
    slots = sources * capacity
    planes = lax.axis_size("dp")
    rows = hidden_width // planes
    me, plane = lax.axis_index("expert"), lax.axis_index("dp")
    bf16 = jnp.bfloat16

    def permute(name, target):
        return lambda x: lax.ppermute(x, name, [(i, target(i)) for i in range(lax.axis_size(name))])

    core = permute("expert", lambda i: i ^ 1)
    first = permute("expert", lambda i: i ^ (4 if i & 1 else 2))
    second = permute("expert", lambda i: i ^ (2 if i & 1 else 4))
    far1, far2 = (permute("dp", lambda i, o=o: i ^ o) for o in (1, 2))
    inner = lambda x: lax.ppermute(x, "dp", [(1, 2), (2, 1)])
    outer = lambda x: lax.ppermute(x, "dp", [(0, 3), (3, 0)])
    outward = lambda x: lax.ppermute(x, "dp", [(1, 0), (2, 3)])
    info = jnp.stack([me, plane]).astype(jnp.int32)
    hidden4 = saved_hidden.reshape(sources // 2, 2, capacity, hidden_width)
    saved4 = saved_output.reshape(sources // 2, 2, capacity, width)

    def shaped(*shape, dtype=bf16):
        return pltpu.VMEM(shape, dtype)

    def fetched(cores):
        return [
            pltpu.VMEM((sources // 2, cores, capacity, width), bf16),
            pltpu.SemaphoreType.DMA((sources // 2, cores)),
        ]

    acc = shaped(rows, width, dtype=jnp.float32)
    flops = 4 * rows * width * 4 * tokens

    def add(hidden, blocks, totals=(), experts=(0, 1), out=acc):
        return call(
            functools.partial(sum_kernel, len(hidden), experts, bool(totals)), [out] * len(experts),
            (info, *hidden, *totals, *blocks), flops=flops * len(experts) // 2,
            aliases={1 + len(hidden) + n: n for n in range(len(totals))} if out is acc else None,
        )

    def choose(inner_block, outer_block, *score):
        extra = META if score else 0
        return call(
            choose_kernel, [shaped(width + META + extra, tokens)], (info, inner_block, outer_block, *score)
        )[0]

    def join(a, b):
        return call(join_kernel, [shaped(2, *a.shape)], (a, b))[0]

    (own,) = call(
        pack_kernel,
        [shaped(width + META, tokens)],
        tuple(x.T[None, None] for x in (out_grad, expert_ids, gate_weight)),
        scratch=[
            pltpu.VMEM(expert_ids.shape[::-1], jnp.int32),
            pltpu.VMEM(gate_weight.shape[::-1], jnp.float32),
            pltpu.SemaphoreType.DMA((3,)),
        ],
    )
    kept, leaving = call(
        turn_kernel, [shaped(hidden_width, slots // 2)] * 2, (info, hidden4), scratch=fetched(2)
    )
    own, leaving = phase(own, leaving)
    near, across, f0, got = far1(own), inner(own), first(own), core(leaving)
    h0, h1, h2, h3 = call(
        quarter_kernel,
        [shaped(rows, slots)] * planes,
        (info, kept, got),
        scratch=[pltpu.VMEM((planes, rows, slots), bf16)],
    )
    s0 = second(join(own, f0))

    (saved_leaving,) = call(
        saved_kernel, [shaped(width * slots // 2 // LANES, LANES)], (after(info, f0), saved4), scratch=fetched(1)
    )
    near, across, h0, saved_leaving = phase(near, across, h0, saved_leaving)
    inside, outside, f1 = inner(near), outward(across), first(near)
    saved_got = core(saved_leaving)
    near, s0 = phase(near, s0)
    s1 = second(join(near, f1))

    inside, outside, h3, saved_got = phase(inside, outside, h3, saved_got)
    third, h3_inner = outward(inside), inner(h3)
    block2 = choose(inside, outside)
    f2 = first(after(block2, s0))
    totals = add((h0,), (own, f0, s0))
    (score,) = call(
        score_kernel, [shaped(8, LANES, dtype=jnp.float32)], (info, saved4, saved_got, own, f0, s0),
        scratch=fetched(1), flops=4 * slots * width * tokens,
    )
    s2 = second(join(block2, f2))

    third, h3_inner, h1, h2, totals, score = phase(third, h3_inner, h1, h2, totals, score)
    h1, h2 = far1(h1), far2(h2)
    block3 = choose(across, third, score)
    f3 = first(after(block3, s1))
    s3 = second(join(block3, f3))

    h1, h2, h3 = phase(h1, h2, h3)
    h3_outer = outer(h3)
    totals = add((h1,), (near, f1, s1), totals)
    totals = add((h2,), (block2, f2, s2), totals)
    blocks3 = (block3, f3, s3)
    last = (h3_inner, h3_outer)
    (leaving_part,) = add(last, blocks3, totals[1:], (1,), shaped(rows, width))
    got_part = core(leaving_part)
    (own_total,) = add(last, blocks3, totals[:1], (0,))
    (down_grad,) = call(add_kernel, [jax.ShapeDtypeStruct((rows, width), bf16)], (own_total, got_part))

    (route_grad,) = call(
        route_kernel,
        [jax.ShapeDtypeStruct((expert_ids.shape[1], tokens), jnp.float32)],
        (info, expert_ids.T[None, None], score, f3, s3),
        scratch=[pltpu.VMEM(expert_ids.shape[::-1], jnp.int32), pltpu.SemaphoreType.DMA],
    )
    return (down_grad.reshape(1, rows, width), route_grad.T)


def fits(mesh, out_grad, expert_ids, gate_weight, saved_hidden, saved_output):
    planes, experts = mesh.shape["dp"], mesh.shape["expert"]
    tokens, width = out_grad.shape[0] // (planes * experts), out_grad.shape[1]
    rest = width % LANES
    return (
        planes == 4
        and experts == 8
        and tokens == LANES
        and 2 * saved_hidden.shape[3] == LANES
        and saved_hidden.shape[4] % (8 * planes) == 0
        and rest > 0
        and rest % 8 == 0
        and LANES % rest == 0
    )


def solution(mesh):
    placed = (
        P(("dp", "expert"), None),
        P(("dp", "expert"), None),
        P(("dp", "expert"), None),
        P("dp", "expert", None, None, None),
        P("dp", "expert", None, None, None),
    )

    def run(*arrays):
        return jax.shard_map(
            planes4 if fits(mesh, *arrays) else general,
            mesh=mesh,
            in_specs=placed,
            out_specs=(P("expert", "dp", None), P(("dp", "expert"), None)),
            check_vma=False,
        )(*arrays)

    return run
```

```python
import functools

import jax
import jax.numpy as jnp
from jax import lax
from jax.experimental import pallas as pl
from jax.experimental.pallas import tpu as pltpu
from jax.sharding import PartitionSpec as P

LANES = 128
META = 16
AFTER = {
    "saved": ("f0",),
    "inside": ("quarters", "saved",),
    "outside": ("near", "saved",),
    "f1": ("across", "saved",),
    "j1": ("s0",),
    "third": ("outside", "saved_swapped",),
    "h3_inner": ("inside", "outside", "saved_swapped", "across",),
    "f2": ("s0",),
    "h1": ("third",),
    "h2": ("h3_inner",),
    "f3": ("s1",),
    "h3_outer": ("h1", "h2",),
    "j3": ("h1",),
    "turned": ("own",),
}
SCALE, SCALES = 3, {"t2": 0.5, "turned": 2, "t0": 0.5}
TOTALS = ("t0", "t1", "t2")
H3 = ("h3_inner", "h3_outer")


def slot_numbers(ids, experts, capacity):
    rows = ids.shape[0] * ids.shape[1]
    flat = (ids.reshape(rows, 1) == jnp.arange(experts, dtype=jnp.int32)[None, :]).astype(jnp.int32)
    earlier = jnp.cumsum(flat, axis=0) - flat
    position = jnp.sum(earlier * flat, axis=1).reshape(ids.shape)
    return ids * capacity + position


def general(out_grad, expert_ids, gate_weight, saved_hidden, saved_output):
    tokens_here, width = out_grad.shape
    experts = lax.axis_size("expert")
    capacity = saved_hidden.shape[3]
    hidden_width = saved_hidden.shape[4]
    sources = saved_hidden.shape[2]
    slot = slot_numbers(expert_ids, experts, capacity)
    table = slot[:, :, None] == jnp.arange(experts * capacity, dtype=jnp.int32)[None, None, :]
    occupancy = jnp.sum(table, axis=1).astype(jnp.bfloat16)
    sent = lax.dot_general(
        occupancy, out_grad, (((0,), (0,)), ((), ())), preferred_element_type=jnp.float32
    )
    sent = sent.astype(jnp.bfloat16).reshape(experts, capacity, width)
    gate_slots = jnp.sum(jnp.where(table, gate_weight[:, :, None], jnp.float32(0.0)), axis=(0, 1))
    gate_slots = gate_slots.reshape(experts, capacity)
    arrived, arrived_gate = (
        lax.all_to_all(sent, "expert", split_axis=0, concat_axis=0, tiled=True),
        lax.all_to_all(
            gate_slots.astype(jnp.bfloat16), "expert", split_axis=0, concat_axis=0, tiled=True
        ).astype(gate_slots.dtype),
    )
    scaled = (
        (arrived_gate[:, :, None] * arrived).astype(jnp.bfloat16).reshape(sources * capacity, width)
    )
    hidden = saved_hidden.reshape(sources * capacity, hidden_width)
    own_rows = hidden_width // lax.axis_size("dp")
    down_grad = lax.psum_scatter(
        lax.dot_general(
            hidden, scaled, (((0,), (0,)), ((), ())), preferred_element_type=jnp.float32
        ).astype(jnp.bfloat16),
        "dp",
        scatter_dimension=0,
        tiled=True,
    ).astype(jnp.float32)
    down_grad = down_grad.astype(jnp.bfloat16).reshape(1, own_rows, width)
    outputs = saved_output.reshape(sources, capacity, width)
    returned = lax.all_to_all(outputs, "expert", split_axis=0, concat_axis=0, tiled=True)
    picked = returned.reshape(experts * capacity, width)[slot.reshape(-1)]
    picked = picked.reshape(tokens_here, expert_ids.shape[1], width)
    route_grad = jnp.einsum("tkd,td->tk", picked, out_grad, preferred_element_type=jnp.float32)
    return (down_grad, route_grad)


def pack_kernel(grad_ref, ids_ref, gate_ref, out_ref, ids, gate, sems):
    width, tokens = grad_ref.shape[2:]
    copies = [
        pltpu.make_async_copy(ids_ref.at[0, 0], ids, sems.at[0]),
        pltpu.make_async_copy(gate_ref.at[0, 0], gate, sems.at[1]),
        pltpu.make_async_copy(grad_ref.at[0, 0], out_ref.at[:width], sems.at[2]),
    ]
    for copy in copies:
        copy.start()
    copies[0].wait()
    copies[1].wait()
    expert = lax.broadcasted_iota(jnp.int32, (META // 2, tokens), 0)
    dense = jnp.zeros((META // 2, tokens), jnp.float32)
    for k in range(ids.shape[0]):
        dense = dense + jnp.where(expert == ids[k:k + 1, :], gate[k:k + 1, :], 0.0)
    high = dense.astype(jnp.bfloat16).astype(jnp.float32)
    out_ref[width:, :] = jnp.concatenate([high, dense - high], axis=0).astype(jnp.bfloat16)
    copies[2].wait()


def fetch(source, target, sems, cores):
    copies = [
        pltpu.make_async_copy(source.at[c, core], target.at[c, n], sems.at[c, n])
        for c in range(source.shape[0])
        for n, core in enumerate(cores)
    ]
    for copy in copies:
        copy.start()
    for copy in copies:
        copy.wait()


def stacked(ref, n, cols):
    return jnp.concatenate([ref[c, n, :, cols] for c in range(ref.shape[0])], axis=0)


def turn_kernel(hidden_ref, keep_ref, leave_ref, here, sems):
    core = lax.axis_index("expert") & 1
    fetch(hidden_ref, here, sems, (core, 1 - core))
    width = here.shape[3]
    for a in range(0, width, LANES):
        cols = slice(a, min(a + LANES, width))
        keep_ref[cols, :] = stacked(here, 0, cols).T
        leave_ref[cols, :] = stacked(here, 1, cols).T


def quarter_kernel(keep_ref, got_ref, *rest):
    outs, scratch = rest[:-1], rest[-1]
    planes, rows, half = len(outs), outs[0].shape[0], keep_ref.shape[1]
    for q in range(planes):
        scratch[q, :, :half] = keep_ref[q * rows:(q + 1) * rows, :]
        scratch[q, :, half:] = got_ref[q * rows:(q + 1) * rows, :]
    for o in range(planes):
        outs[o][...] = scratch[lax.axis_index("dp") ^ o]


def saved_kernel(saved_ref, out_ref, here, sems):
    fetch(saved_ref, here, sems, (1 - (lax.axis_index("expert") & 1),))
    rows, width = here.shape[0] * here.shape[2], here.shape[3]
    full, rest = width // LANES, width % LANES
    for j in range(full):
        out_ref[j * rows:(j + 1) * rows, :] = stacked(here, 0, slice(j * LANES, (j + 1) * LANES))
    tail = stacked(here, 0, slice(full * LANES, width)).astype(jnp.float32)
    step = rows * rest // LANES
    out_ref[full * rows:, :] = jnp.concatenate(
        [tail[a * step:(a + 1) * step] for a in range(LANES // rest)], axis=1
    ).astype(jnp.bfloat16)


def choose_kernel(inner_ref, outer_ref, *refs):
    out_ref = refs[-1]
    rows = inner_ref.shape[0]
    plane = lax.axis_index("dp")
    middle = jnp.logical_or(plane == 1, plane == 2)

    @pl.when(middle)
    def _():
        out_ref[:rows, :] = inner_ref[...]

    @pl.when(jnp.logical_not(middle))
    def _():
        out_ref[:rows, :] = outer_ref[...]

    if len(refs) > 1:
        score = refs[0][...]
        high = score.astype(jnp.bfloat16).astype(jnp.float32)
        out_ref[rows:, :] = jnp.concatenate([high, score - high], axis=0).astype(jnp.bfloat16)


def join_kernel(a_ref, b_ref, out_ref):
    out_ref[0] = a_ref[...]
    out_ref[1] = b_ref[...]


def block_tables(blocks, width):
    me = lax.axis_index("expert")
    core, chip = me & 1, me >> 1
    offsets = [0, 1 + core, 2 - core, 3]
    rows = lax.broadcasted_iota(jnp.int32, (META, LANES), 0)
    metas = [ref[width:width + META, :].astype(jnp.float32) for ref in blocks]
    gates = []
    for expert in (me, me ^ 1):
        picked = jnp.logical_or(rows == expert, rows == expert + META // 2)
        gates += [jnp.sum(jnp.where(picked, meta, 0.0), axis=0, keepdims=True) for meta in metas]
    gates = jnp.concatenate(gates, axis=0)
    routed = gates > 0.0
    before = lax.broadcasted_iota(jnp.int32, (LANES, LANES), 0) < lax.broadcasted_iota(jnp.int32, (LANES, LANES), 1)
    earlier = jnp.dot(
        routed.astype(jnp.bfloat16), before.astype(jnp.bfloat16), preferred_element_type=jnp.float32
    ).astype(jnp.int32)
    position = jnp.where(routed, earlier, -LANES * LANES)
    number = len(blocks)
    out = []
    for w in range(2):
        gate = jnp.concatenate([gates[w * number + n:w * number + n + 1] for n in range(number)], axis=1)
        place = jnp.concatenate(
            [position[w * number + n:w * number + n + 1] + (chip ^ offsets[n]) * (LANES // 2) for n in range(number)],
            axis=1,
        )
        out.append((gate, place))
    return out


def chosen(place, slots):
    return lax.broadcasted_iota(jnp.int32, (slots, place.shape[1]), 0) == place


def gather_hidden(hidden, table):
    gate, place = table
    placed = jnp.dot(
        hidden, chosen(place, hidden.shape[1]).astype(jnp.bfloat16), preferred_element_type=jnp.float32
    )
    return (placed * gate).astype(jnp.bfloat16)


def chunks(width, step=2 * LANES):
    return [(a, min(a + step, width)) for a in range(0, width, step)]


def tokens_of(blocks, a, b):
    return jnp.concatenate([ref[a:b, :] for ref in blocks], axis=1)


def four(refs):
    own, first, pair = refs
    return [own, first, pair.at[0], pair.at[1]]


def sum_kernel(choices, experts, started, *refs):
    number = len(experts)
    outs, refs = refs[-number:], refs[:-number]
    accs, refs = (refs[:number], refs[number:]) if started else ((), refs)
    rows, width = outs[0].shape
    plane = lax.axis_index("dp")
    middle = jnp.logical_or(plane == 1, plane == 2)
    replicas = []
    for many in choices:
        hidden_refs, blocks, refs = refs[:many], four(refs[many:many + 3]), refs[many + 3:]
        tables = block_tables(blocks, width)
        half = hidden_refs[0].shape[1] // 2
        hidden = []
        for w in experts:
            parts = [ref[:, w * half:(w + 1) * half] for ref in hidden_refs]
            hidden.append(gather_hidden(parts[0] if many == 1 else jnp.where(middle, *parts), tables[w]))
        replicas.append((hidden[0] if number == 1 else jnp.concatenate(hidden, axis=0), blocks))
    for a, b in chunks(width):
        total = None
        for hidden, blocks in replicas:
            product = lax.dot_general(
                hidden, tokens_of(blocks, a, b), (((1,), (1,)), ((), ())), preferred_element_type=jnp.float32
            )
            total = product if total is None else total + product
        for w, out_ref in enumerate(outs):
            value = total[w * rows:(w + 1) * rows]
            if started:
                value = value + accs[w][:, a:b]
            out_ref[:, a:b] = value.astype(out_ref.dtype)


def score_kernel(saved_ref, got_ref, *refs):
    blocks, (score_ref, here, sems) = four(refs[:-3]), refs[-3:]
    fetch(saved_ref, here, sems, (lax.axis_index("expert") & 1,))
    rows, width = here.shape[0] * here.shape[2], here.shape[3]
    tables = block_tables(blocks, width)
    full, rest = width // LANES, width % LANES
    total = jnp.zeros((2 * rows, len(blocks) * LANES), jnp.float32)
    for a, b in chunks(width):
        pieces = []
        for j in range(a // LANES, -(-b // LANES)):
            if j < full:
                pieces.append(got_ref[j * rows:(j + 1) * rows, :])
            else:
                tail = got_ref[full * rows:, :]
                pieces.append(
                    jnp.concatenate([tail[:, n * rest:(n + 1) * rest] for n in range(LANES // rest)], axis=0)
                )
        theirs = pieces[0] if len(pieces) == 1 else jnp.concatenate(pieces, axis=1)
        saved = jnp.concatenate([stacked(here, 0, slice(a, b)), theirs], axis=0)
        total = total + jnp.dot(saved, tokens_of(blocks, a, b), preferred_element_type=jnp.float32)
    scores = []
    for w in range(2):
        row = jnp.sum(
            jnp.where(chosen(tables[w][1], rows), total[w * rows:(w + 1) * rows], 0.0), axis=0, keepdims=True
        )
        scores += [row[:, n * LANES:(n + 1) * LANES] for n in range(len(blocks))]
    score_ref[...] = jnp.concatenate(scores, axis=0)


def route_kernel(ids_ref, score_ref, first_ref, pair_ref, out_ref, ids, sem):
    copy = pltpu.make_async_copy(ids_ref.at[0, 0], ids, sem)
    copy.start()
    half = META // 2
    parts = [score_ref[...]]
    for ref in (first_ref, pair_ref.at[0], pair_ref.at[1]):
        sent = ref[ref.shape[0] - META:, :].astype(jnp.float32)
        parts.append(sent[:half] + sent[half:])
    me = lax.axis_index("expert")
    core = me & 1
    offsets = [0, 2 + 2 * core, 4 - 2 * core, 6]
    copy.wait()
    wanted = ids[...] ^ me
    total = jnp.zeros(wanted.shape, jnp.float32)
    for w in range(2):
        for n, part in enumerate(parts):
            total = total + jnp.where(wanted == offsets[n] ^ w, part[4 * w + n:4 * w + n + 1], 0.0)
    out_ref[...] = total


def add_kernel(a_ref, b_ref, out_ref):
    out_ref[...] = (a_ref[...] + b_ref[...].astype(jnp.float32)).astype(out_ref.dtype)


def call(kernel, outs, args, scratch=(), flops=0, limit=8, aliases=None, name=None):
    smem, vmem, hbm = (pl.BlockSpec(memory_space=space) for space in (pltpu.SMEM, pltpu.VMEM, pltpu.HBM))
    moved = sum(a.size * a.dtype.itemsize for a in args)
    scale = SCALES.get(name, SCALE)
    specs, operands = [], []
    for a in args:
        specs.append(hbm if a.ndim == 4 else vmem)
        if a.ndim > 1:
            a = pltpu.with_memory_space_constraint(a, pltpu.HBM if a.ndim == 4 else pltpu.VMEM)
        operands.append(a)
    return pl.pallas_call(
        kernel,
        out_shape=outs,
        in_specs=specs,
        out_specs=[vmem] * len(outs),
        scratch_shapes=list(scratch),
        input_output_aliases=aliases or {},
        compiler_params=pltpu.CompilerParams(vmem_limit_bytes=limit * 1024 * 1024),
        cost_estimate=pl.CostEstimate(flops=int(scale * flops), bytes_accessed=int(scale * moved), transcendentals=0),
    )(*operands)


def phase(*values):
    return lax.optimization_barrier(values)


def after(value, *earlier):
    return phase(value, *earlier)[0]


def planes4(out_grad, expert_ids, gate_weight, saved_hidden, saved_output):
    tokens, width = out_grad.shape
    hidden_width = saved_hidden.shape[4]
    sources, capacity = saved_hidden.shape[2:4]
    slots = sources * capacity
    planes = lax.axis_size("dp")
    rows = hidden_width // planes
    bf16 = jnp.bfloat16

    def permute(name, target):
        return lambda x: lax.ppermute(x, name, [(i, target(i)) for i in range(lax.axis_size(name))])

    core = permute("expert", lambda i: i ^ 1)
    first = permute("expert", lambda i: i ^ (4 if i & 1 else 2))
    second = permute("expert", lambda i: i ^ (2 if i & 1 else 4))
    far1, far2, far3 = (permute("dp", lambda i, o=o: i ^ o) for o in (1, 2, 3))
    inner = lambda x: lax.ppermute(x, "dp", [(1, 2), (2, 1)])
    outer = lambda x: lax.ppermute(x, "dp", [(0, 3), (3, 0)])
    outward = lambda x: lax.ppermute(x, "dp", [(1, 0), (2, 3)])
    hidden4 = saved_hidden.reshape(sources // 2, 2, capacity, hidden_width)
    saved4 = saved_output.reshape(sources // 2, 2, capacity, width)

    def shaped(*shape, dtype=bf16):
        return pltpu.VMEM(shape, dtype)

    def fetched(cores):
        return [
            pltpu.VMEM((sources // 2, cores, capacity, width), bf16),
            pltpu.SemaphoreType.DMA((sources // 2, cores)),
        ]

    acc = shaped(rows, width, dtype=jnp.float32)
    flops = 4 * rows * width * 4 * tokens

    def add(replicas, totals=(), experts=(0, 1), out=acc, name=None):
        arrays = [x for hidden, blocks in replicas for x in (*hidden, *blocks)]
        return call(
            functools.partial(sum_kernel, [len(hidden) for hidden, blocks in replicas], experts, bool(totals)),
            [out] * len(experts),
            (*totals, *arrays), flops=flops * len(replicas) * len(experts) // 2, name=name,
            aliases={n: n for n in range(len(totals))} if out is acc else None,
        )

    def choose(inner_block, outer_block, *score):
        extra = META if score else 0
        return call(
            choose_kernel, [shaped(width + META + extra, tokens)], (inner_block, outer_block, *score)
        )[0]

    def join(a, b):
        return call(join_kernel, [shaped(2, *a.shape)], (a, b))[0]

    steps = {
        "hidden": (lambda: hidden4,),
        "outputs": (lambda: saved4,),
        "own": (
            lambda: call(
                pack_kernel,
                [shaped(width + META, tokens)],
                tuple(x.T[None, None] for x in (out_grad, expert_ids, gate_weight)),
                scratch=[
                    pltpu.VMEM(expert_ids.shape[::-1], jnp.int32),
                    pltpu.VMEM(gate_weight.shape[::-1], jnp.float32),
                    pltpu.SemaphoreType.DMA((3,)),
                ],
                name="own",
            )[0],
        ),
        "turned": (
            lambda x: call(
                turn_kernel, [shaped(hidden_width, slots // 2)] * 2, (x,), scratch=fetched(2), name="turned"
            ),
            "hidden",
        ),
        "swapped": (lambda t: core(t[1]), "turned"),
        "quarters": (
            lambda t, got: call(
                quarter_kernel,
                [shaped(rows, slots)] * planes,
                (t[0], got),
                scratch=[pltpu.VMEM((planes, rows, slots), bf16)],
                name="quarters",
            ),
            "turned", "swapped",
        ),
        "h1": (lambda h: far1(h[1]), "quarters"),
        "h2": (lambda h: far2(h[2]), "quarters"),
        "h3": (lambda h: far3(h[3]), "quarters"),
        "h3_inner": (lambda h: inner(h[3]), "quarters"),
        "h3_outer": (lambda h: outer(h[3]), "quarters"),
        "near": (far1, "own"),
        "across": (inner, "own"),
        "inside": (inner, "near"),
        "outside": (outward, "across"),
        "third": (outward, "inside"),
        "block2": (choose, "inside", "outside"),
        "block3": (choose, "across", "third", "score"),
        "f0": (first, "own"),
        "j0": (join, "own", "f0"),
        "s0": (second, "j0"),
        "f1": (first, "near"),
        "j1": (join, "near", "f1"),
        "s1": (second, "j1"),
        "f2": (first, "block2"),
        "j2": (join, "block2", "f2"),
        "s2": (second, "j2"),
        "f3": (first, "block3"),
        "j3": (join, "block3", "f3"),
        "s3": (second, "j3"),
        "saved": (
            lambda x: call(
                saved_kernel, [shaped(width * slots // 2 // LANES, LANES)], (x,), scratch=fetched(1), name="saved"
            )[0],
            "outputs",
        ),
        "saved_swapped": (core, "saved"),
        "score": (
            lambda got, *blocks: call(
                score_kernel, [shaped(8, LANES, dtype=jnp.float32)], (saved4, got, *blocks),
                scratch=fetched(1), flops=4 * slots * width * tokens, name="score",
            )[0],
            "saved_swapped", "own", "f0", "s0",
        ),
        "part_swapped": (core, "part"),
        "down": (
            lambda a, b: call(add_kernel, [jax.ShapeDtypeStruct((rows, width), bf16)], (a, b), name="down")[0],
            "mine", "part_swapped",
        ),
        "route": (
            lambda *scores: call(
                route_kernel,
                [jax.ShapeDtypeStruct((expert_ids.shape[1], tokens), jnp.float32)],
                (expert_ids.T[None, None], *scores),
                scratch=[pltpu.VMEM(expert_ids.shape[::-1], jnp.int32), pltpu.SemaphoreType.DMA],
                name="route",
            )[0],
            "score", "f3", "s3",
        ),
    }
    sums = {
        "t0": ("quarters", "own", "f0", "s0"),
        "t1": ("h1", "near", "f1", "s1"),
        "t2": ("h2", "block2", "f2", "s2"),
        "t3": (*H3, "block3", "f3", "s3"),
    }

    def split(names, values):
        replicas = []
        for n in names:
            many = len(sums[n]) - 3
            hidden = (values[0][0],) if n == "t0" else values[:many]
            replicas.append((hidden, values[many:many + 3]))
            values = values[many + 3:]
        return replicas

    before = None
    for n in TOTALS:
        build = lambda *values, n=n, started=before is not None: add(
            split([n], values[1:] if started else values), values[0] if started else (), name=n
        )
        steps[n] = (build, *([before] if before else []), *sums[n])
        before = n
    late = [n for n in sums if n not in TOTALS]
    for n, experts, out in (("part", (1,), shaped(rows, width)), ("mine", (0,), acc)):
        build = lambda t, *values, n=n, experts=experts, out=out: add(
            split(late, values), [t[w] for w in experts], experts, out, name=n
        )[0]
        steps[n] = (build, before, *(x for m in late for x in sums[m]))
    made = {}

    def get(name):
        if name not in made:
            build, *needs = steps[name]
            values = [get(other) for other in needs]
            earlier = [get(other) for other in AFTER.get(name, ())]
            if earlier:
                values = phase(*values, *earlier)[:len(values)]
            made[name] = build(*values)
        return made[name]

    return (get("down").reshape(1, rows, width), get("route").T)


def fits(mesh, out_grad, expert_ids, gate_weight, saved_hidden, saved_output):
    planes, experts = mesh.shape["dp"], mesh.shape["expert"]
    tokens, width = out_grad.shape[0] // (planes * experts), out_grad.shape[1]
    rest = width % LANES
    return (
        planes == 4
        and experts == 8
        and tokens == LANES
        and 2 * saved_hidden.shape[3] == LANES
        and saved_hidden.shape[4] % (8 * planes) == 0
        and rest > 0
        and rest % 8 == 0
        and LANES % rest == 0
    )


def solution(mesh):
    placed = (
        P(("dp", "expert"), None),
        P(("dp", "expert"), None),
        P(("dp", "expert"), None),
        P("dp", "expert", None, None, None),
        P("dp", "expert", None, None, None),
    )

    def run(*arrays):
        return jax.shard_map(
            planes4 if fits(mesh, *arrays) else general,
            mesh=mesh,
            in_specs=placed,
            out_specs=(P("expert", "dp", None), P(("dp", "expert"), None)),
            check_vma=False,
        )(*arrays)

    return run
```

```python
import functools

import jax
import jax.numpy as jnp
from jax import lax
from jax.experimental import pallas as pl
from jax.experimental.pallas import tpu as pltpu
from jax.sharding import PartitionSpec as P

LANES = 128
META = 16
AFTER = {
    "saved": ("f0",),
    "inside": ("quarters", "saved",),
    "outside": ("near", "saved",),
    "f1": ("across", "saved",),
    "j1": ("s0",),
    "third": ("outside", "saved_swapped",),
    "h3_inner": ("inside", "outside", "across",),
    "f2": ("s0",),
    "h1": ("third",),
    "h2": ("h3_inner",),
    "f3": ("s1",),
    "h3_outer": ("h1", "h2",),
    "j3": ("h1",),
    "turned": ("own",),
}
SCALE, SCALES = 3, {"t2": 0.5, "turned": 2, "t0": 0.5, "own": 40}
TOTALS = ("t0", "t1", "t2")
H3 = ("h3_inner", "h3_outer")


def slot_numbers(ids, experts, capacity):
    rows = ids.shape[0] * ids.shape[1]
    flat = (ids.reshape(rows, 1) == jnp.arange(experts, dtype=jnp.int32)[None, :]).astype(jnp.int32)
    earlier = jnp.cumsum(flat, axis=0) - flat
    position = jnp.sum(earlier * flat, axis=1).reshape(ids.shape)
    return ids * capacity + position


def general(out_grad, expert_ids, gate_weight, saved_hidden, saved_output):
    tokens_here, width = out_grad.shape
    experts = lax.axis_size("expert")
    capacity = saved_hidden.shape[3]
    hidden_width = saved_hidden.shape[4]
    sources = saved_hidden.shape[2]
    slot = slot_numbers(expert_ids, experts, capacity)
    table = slot[:, :, None] == jnp.arange(experts * capacity, dtype=jnp.int32)[None, None, :]
    occupancy = jnp.sum(table, axis=1).astype(jnp.bfloat16)
    sent = lax.dot_general(
        occupancy, out_grad, (((0,), (0,)), ((), ())), preferred_element_type=jnp.float32
    )
    sent = sent.astype(jnp.bfloat16).reshape(experts, capacity, width)
    gate_slots = jnp.sum(jnp.where(table, gate_weight[:, :, None], jnp.float32(0.0)), axis=(0, 1))
    gate_slots = gate_slots.reshape(experts, capacity)
    arrived, arrived_gate = (
        lax.all_to_all(sent, "expert", split_axis=0, concat_axis=0, tiled=True),
        lax.all_to_all(
            gate_slots.astype(jnp.bfloat16), "expert", split_axis=0, concat_axis=0, tiled=True
        ).astype(gate_slots.dtype),
    )
    scaled = (
        (arrived_gate[:, :, None] * arrived).astype(jnp.bfloat16).reshape(sources * capacity, width)
    )
    hidden = saved_hidden.reshape(sources * capacity, hidden_width)
    own_rows = hidden_width // lax.axis_size("dp")
    down_grad = lax.psum_scatter(
        lax.dot_general(
            hidden, scaled, (((0,), (0,)), ((), ())), preferred_element_type=jnp.float32
        ).astype(jnp.bfloat16),
        "dp",
        scatter_dimension=0,
        tiled=True,
    ).astype(jnp.float32)
    down_grad = down_grad.astype(jnp.bfloat16).reshape(1, own_rows, width)
    outputs = saved_output.reshape(sources, capacity, width)
    returned = lax.all_to_all(outputs, "expert", split_axis=0, concat_axis=0, tiled=True)
    picked = returned.reshape(experts * capacity, width)[slot.reshape(-1)]
    picked = picked.reshape(tokens_here, expert_ids.shape[1], width)
    route_grad = jnp.einsum("tkd,td->tk", picked, out_grad, preferred_element_type=jnp.float32)
    return (down_grad, route_grad)


def pack_kernel(grad_ref, ids_ref, gate_ref, out_ref, ids, gate, sems):
    width, tokens = grad_ref.shape[2:]
    copies = [
        pltpu.make_async_copy(ids_ref.at[0, 0], ids, sems.at[0]),
        pltpu.make_async_copy(gate_ref.at[0, 0], gate, sems.at[1]),
        pltpu.make_async_copy(grad_ref.at[0, 0], out_ref.at[:width], sems.at[2]),
    ]
    for copy in copies:
        copy.start()
    copies[0].wait()
    copies[1].wait()
    expert = lax.broadcasted_iota(jnp.int32, (META // 2, tokens), 0)
    dense = jnp.zeros((META // 2, tokens), jnp.float32)
    for k in range(ids.shape[0]):
        dense = dense + jnp.where(expert == ids[k:k + 1, :], gate[k:k + 1, :], 0.0)
    high = dense.astype(jnp.bfloat16).astype(jnp.float32)
    out_ref[width:, :] = jnp.concatenate([high, dense - high], axis=0).astype(jnp.bfloat16)
    copies[2].wait()


def fetch(source, target, sems, cores):
    copies = [
        [pltpu.make_async_copy(source.at[c, core], target.at[c, n], sems.at[c, n]) for n, core in enumerate(cores)]
        for c in range(source.shape[0])
    ]
    for chip in copies:
        for copy in chip:
            copy.start()
    return copies


def arrive(copies):
    for chip in copies:
        for copy in chip:
            copy.wait()


def stacked(ref, n, cols, chips):
    return jnp.concatenate([ref[c, n, :, cols] for c in chips], axis=0)


def turn_kernel(hidden_ref, keep_ref, leave_ref, here, sems):
    core = lax.axis_index("expert") & 1
    copies = fetch(hidden_ref, here, sems, (core, 1 - core))
    width, pair = here.shape[3], 2 * here.shape[2]
    for c in range(0, here.shape[0], 2):
        arrive(copies[c:c + 2])
        to = slice(c // 2 * pair, (c // 2 + 1) * pair)
        for a in range(0, width, LANES):
            cols = slice(a, min(a + LANES, width))
            keep_ref[cols, to] = stacked(here, 0, cols, (c, c + 1)).T
            leave_ref[cols, to] = stacked(here, 1, cols, (c, c + 1)).T


def quarter_kernel(keep_ref, got_ref, *rest):
    outs, scratch = rest[:-1], rest[-1]
    planes, rows, half = len(outs), outs[0].shape[0], keep_ref.shape[1]
    for q in range(planes):
        scratch[q, :, :half] = keep_ref[q * rows:(q + 1) * rows, :]
        scratch[q, :, half:] = got_ref[q * rows:(q + 1) * rows, :]
    for o in range(planes):
        outs[o][...] = scratch[lax.axis_index("dp") ^ o]


def saved_kernel(saved_ref, out_ref, here, sems):
    arrive(fetch(saved_ref, here, sems, (1 - (lax.axis_index("expert") & 1),)))
    chips = range(here.shape[0])
    rows, width = here.shape[0] * here.shape[2], here.shape[3]
    full, rest = width // LANES, width % LANES
    for j in range(full):
        out_ref[j * rows:(j + 1) * rows, :] = stacked(here, 0, slice(j * LANES, (j + 1) * LANES), chips)
    tail = stacked(here, 0, slice(full * LANES, width), chips).astype(jnp.float32)
    step = rows * rest // LANES
    out_ref[full * rows:, :] = jnp.concatenate(
        [tail[a * step:(a + 1) * step] for a in range(LANES // rest)], axis=1
    ).astype(jnp.bfloat16)


def choose_kernel(inner_ref, outer_ref, *refs):
    out_ref = refs[-1]
    rows = inner_ref.shape[0]
    plane = lax.axis_index("dp")
    middle = jnp.logical_or(plane == 1, plane == 2)

    @pl.when(middle)
    def _():
        out_ref[:rows, :] = inner_ref[...]

    @pl.when(jnp.logical_not(middle))
    def _():
        out_ref[:rows, :] = outer_ref[...]

    if len(refs) > 1:
        score = refs[0][...]
        high = score.astype(jnp.bfloat16).astype(jnp.float32)
        out_ref[rows:, :] = jnp.concatenate([high, score - high], axis=0).astype(jnp.bfloat16)


def join_kernel(a_ref, b_ref, out_ref):
    out_ref[0] = a_ref[...]
    out_ref[1] = b_ref[...]


def block_tables(blocks, width):
    me = lax.axis_index("expert")
    core, chip = me & 1, me >> 1
    offsets = [0, 1 + core, 2 - core, 3]
    rows = lax.broadcasted_iota(jnp.int32, (META, LANES), 0)
    metas = [ref[width:width + META, :].astype(jnp.float32) for ref in blocks]
    gates = []
    for expert in (me, me ^ 1):
        picked = jnp.logical_or(rows == expert, rows == expert + META // 2)
        gates += [jnp.sum(jnp.where(picked, meta, 0.0), axis=0, keepdims=True) for meta in metas]
    gates = jnp.concatenate(gates, axis=0)
    routed = gates > 0.0
    before = lax.broadcasted_iota(jnp.int32, (LANES, LANES), 0) < lax.broadcasted_iota(jnp.int32, (LANES, LANES), 1)
    earlier = jnp.dot(
        routed.astype(jnp.bfloat16), before.astype(jnp.bfloat16), preferred_element_type=jnp.float32
    ).astype(jnp.int32)
    position = jnp.where(routed, earlier, -LANES * LANES)
    number = len(blocks)
    out = []
    for w in range(2):
        gate = jnp.concatenate([gates[w * number + n:w * number + n + 1] for n in range(number)], axis=1)
        place = jnp.concatenate(
            [position[w * number + n:w * number + n + 1] + (chip ^ offsets[n]) * (LANES // 2) for n in range(number)],
            axis=1,
        )
        out.append((gate, place))
    return out


def chosen(place, slots):
    return lax.broadcasted_iota(jnp.int32, (slots, place.shape[1]), 0) == place


def gather_hidden(hidden, table):
    gate, place = table
    placed = jnp.dot(
        hidden, chosen(place, hidden.shape[1]).astype(jnp.bfloat16), preferred_element_type=jnp.float32
    )
    return (placed * gate).astype(jnp.bfloat16)


def chunks(width, step=2 * LANES):
    return [(a, min(a + step, width)) for a in range(0, width, step)]


def tokens_of(blocks, a, b):
    return jnp.concatenate([ref[a:b, :] for ref in blocks], axis=1)


def four(refs):
    own, first, pair = refs
    return [own, first, pair.at[0], pair.at[1]]


def sum_kernel(choices, experts, started, *refs):
    number = len(experts)
    outs, refs = refs[-number:], refs[:-number]
    accs, refs = (refs[:number], refs[number:]) if started else ((), refs)
    rows, width = outs[0].shape
    plane = lax.axis_index("dp")
    middle = jnp.logical_or(plane == 1, plane == 2)
    replicas = []
    for many in choices:
        hidden_refs, blocks, refs = refs[:many], four(refs[many:many + 3]), refs[many + 3:]
        tables = block_tables(blocks, width)
        half = hidden_refs[0].shape[1] // 2
        hidden = []
        for w in experts:
            parts = [ref[:, w * half:(w + 1) * half] for ref in hidden_refs]
            hidden.append(gather_hidden(parts[0] if many == 1 else jnp.where(middle, *parts), tables[w]))
        replicas.append((hidden[0] if number == 1 else jnp.concatenate(hidden, axis=0), blocks))
    for a, b in chunks(width):
        total = None
        for hidden, blocks in replicas:
            product = lax.dot_general(
                hidden, tokens_of(blocks, a, b), (((1,), (1,)), ((), ())), preferred_element_type=jnp.float32
            )
            total = product if total is None else total + product
        for w, out_ref in enumerate(outs):
            value = total[w * rows:(w + 1) * rows]
            if started:
                value = value + accs[w][:, a:b]
            out_ref[:, a:b] = value.astype(out_ref.dtype)


def score_kernel(saved_ref, got_ref, *refs):
    blocks, (score_ref, here, sems) = four(refs[:-3]), refs[-3:]
    copies = fetch(saved_ref, here, sems, (lax.axis_index("expert") & 1,))
    chips = range(here.shape[0])
    rows, width = here.shape[0] * here.shape[2], here.shape[3]
    tables = block_tables(blocks, width)
    arrive(copies)
    full, rest = width // LANES, width % LANES
    total = jnp.zeros((2 * rows, len(blocks) * LANES), jnp.float32)
    for a, b in chunks(width):
        pieces = []
        for j in range(a // LANES, -(-b // LANES)):
            if j < full:
                pieces.append(got_ref[j * rows:(j + 1) * rows, :])
            else:
                tail = got_ref[full * rows:, :]
                pieces.append(
                    jnp.concatenate([tail[:, n * rest:(n + 1) * rest] for n in range(LANES // rest)], axis=0)
                )
        theirs = pieces[0] if len(pieces) == 1 else jnp.concatenate(pieces, axis=1)
        saved = jnp.concatenate([stacked(here, 0, slice(a, b), chips), theirs], axis=0)
        total = total + jnp.dot(saved, tokens_of(blocks, a, b), preferred_element_type=jnp.float32)
    scores = []
    for w in range(2):
        row = jnp.sum(
            jnp.where(chosen(tables[w][1], rows), total[w * rows:(w + 1) * rows], 0.0), axis=0, keepdims=True
        )
        scores += [row[:, n * LANES:(n + 1) * LANES] for n in range(len(blocks))]
    score_ref[...] = jnp.concatenate(scores, axis=0)


def route_kernel(ids_ref, score_ref, first_ref, pair_ref, out_ref, ids, sem):
    copy = pltpu.make_async_copy(ids_ref.at[0, 0], ids, sem)
    copy.start()
    half = META // 2
    parts = [score_ref[...]]
    for ref in (first_ref, pair_ref.at[0], pair_ref.at[1]):
        sent = ref[ref.shape[0] - META:, :].astype(jnp.float32)
        parts.append(sent[:half] + sent[half:])
    me = lax.axis_index("expert")
    core = me & 1
    offsets = [0, 2 + 2 * core, 4 - 2 * core, 6]
    copy.wait()
    wanted = ids[...] ^ me
    total = jnp.zeros(wanted.shape, jnp.float32)
    for w in range(2):
        for n, part in enumerate(parts):
            total = total + jnp.where(wanted == offsets[n] ^ w, part[4 * w + n:4 * w + n + 1], 0.0)
    out_ref[...] = total


def add_kernel(a_ref, b_ref, out_ref, total, sems):
    copies = []
    for n, (a, b) in enumerate(chunks(a_ref.shape[1], 4 * LANES)):
        total[:, a:b] = (a_ref[:, a:b] + b_ref[:, a:b].astype(jnp.float32)).astype(total.dtype)
        copies.append(pltpu.make_async_copy(total.at[:, a:b], out_ref.at[:, a:b], sems.at[n]))
        copies[-1].start()
    for copy in copies:
        copy.wait()


def call(kernel, outs, args, scratch=(), flops=0, limit=8, aliases=None, name=None, out_space=pltpu.VMEM):
    vmem, hbm = (pl.BlockSpec(memory_space=space) for space in (pltpu.VMEM, pltpu.HBM))
    moved = sum(a.size * a.dtype.itemsize for a in args)
    scale = SCALES.get(name, SCALE)
    specs, operands = [], []
    for a in args:
        specs.append(hbm if a.ndim == 4 else vmem)
        if a.ndim > 1:
            a = pltpu.with_memory_space_constraint(a, pltpu.HBM if a.ndim == 4 else pltpu.VMEM)
        operands.append(a)
    return pl.pallas_call(
        kernel,
        out_shape=outs,
        in_specs=specs,
        out_specs=[pl.BlockSpec(memory_space=out_space)] * len(outs),
        scratch_shapes=list(scratch),
        input_output_aliases=aliases or {},
        compiler_params=pltpu.CompilerParams(vmem_limit_bytes=limit * 1024 * 1024),
        cost_estimate=pl.CostEstimate(flops=int(scale * flops), bytes_accessed=int(scale * moved), transcendentals=0),
    )(*operands)


def phase(*values):
    return lax.optimization_barrier(values)


def after(value, *earlier):
    return phase(value, *earlier)[0]


def planes4(out_grad, expert_ids, gate_weight, saved_hidden, saved_output):
    tokens, width = out_grad.shape
    hidden_width = saved_hidden.shape[4]
    sources, capacity = saved_hidden.shape[2:4]
    slots = sources * capacity
    planes = lax.axis_size("dp")
    rows = hidden_width // planes
    bf16 = jnp.bfloat16

    def permute(name, target):
        return lambda x: lax.ppermute(x, name, [(i, target(i)) for i in range(lax.axis_size(name))])

    core = permute("expert", lambda i: i ^ 1)
    first = permute("expert", lambda i: i ^ (4 if i & 1 else 2))
    second = permute("expert", lambda i: i ^ (2 if i & 1 else 4))
    far1, far2, far3 = (permute("dp", lambda i, o=o: i ^ o) for o in (1, 2, 3))
    inner = lambda x: lax.ppermute(x, "dp", [(1, 2), (2, 1)])
    outer = lambda x: lax.ppermute(x, "dp", [(0, 3), (3, 0)])
    outward = lambda x: lax.ppermute(x, "dp", [(1, 0), (2, 3)])
    hidden4 = saved_hidden.reshape(sources // 2, 2, capacity, hidden_width)
    saved4 = saved_output.reshape(sources // 2, 2, capacity, width)

    def shaped(*shape, dtype=bf16):
        return pltpu.VMEM(shape, dtype)

    def fetched(cores):
        return [
            pltpu.VMEM((sources // 2, cores, capacity, width), bf16),
            pltpu.SemaphoreType.DMA((sources // 2, cores)),
        ]

    acc = shaped(rows, width, dtype=jnp.float32)
    flops = 4 * rows * width * 4 * tokens

    def add(replicas, totals=(), experts=(0, 1), out=acc, name=None):
        arrays = [x for hidden, blocks in replicas for x in (*hidden, *blocks)]
        return call(
            functools.partial(sum_kernel, [len(hidden) for hidden, blocks in replicas], experts, bool(totals)),
            [out] * len(experts),
            (*totals, *arrays), flops=flops * len(replicas) * len(experts) // 2, name=name,
            aliases={n: n for n in range(len(totals))} if out is acc else None,
        )

    def choose(inner_block, outer_block, *score):
        extra = META if score else 0
        return call(
            choose_kernel, [shaped(width + META + extra, tokens)], (inner_block, outer_block, *score)
        )[0]

    def join(a, b):
        return call(join_kernel, [shaped(2, *a.shape)], (a, b))[0]

    steps = {
        "hidden": (lambda: hidden4,),
        "outputs": (lambda: saved4,),
        "own": (
            lambda: call(
                pack_kernel,
                [shaped(width + META, tokens)],
                tuple(x.T[None, None] for x in (out_grad, expert_ids, gate_weight)),
                scratch=[
                    pltpu.VMEM(expert_ids.shape[::-1], jnp.int32),
                    pltpu.VMEM(gate_weight.shape[::-1], jnp.float32),
                    pltpu.SemaphoreType.DMA((3,)),
                ],
                name="own",
            )[0],
        ),
        "turned": (
            lambda x: call(
                turn_kernel, [shaped(hidden_width, slots // 2)] * 2, (x,), scratch=fetched(2), name="turned"
            ),
            "hidden",
        ),
        "swapped": (lambda t: core(t[1]), "turned"),
        "quarters": (
            lambda t, got: call(
                quarter_kernel,
                [shaped(rows, slots)] * planes,
                (t[0], got),
                scratch=[pltpu.VMEM((planes, rows, slots), bf16)],
                name="quarters",
            ),
            "turned", "swapped",
        ),
        "h1": (lambda h: far1(h[1]), "quarters"),
        "h2": (lambda h: far2(h[2]), "quarters"),
        "h3": (lambda h: far3(h[3]), "quarters"),
        "h3_inner": (lambda h: inner(h[3]), "quarters"),
        "h3_outer": (lambda h: outer(h[3]), "quarters"),
        "near": (far1, "own"),
        "across": (inner, "own"),
        "inside": (inner, "near"),
        "outside": (outward, "across"),
        "third": (outward, "inside"),
        "block2": (choose, "inside", "outside"),
        "block3": (choose, "across", "third", "score"),
        "f0": (first, "own"),
        "j0": (join, "own", "f0"),
        "s0": (second, "j0"),
        "f1": (first, "near"),
        "j1": (join, "near", "f1"),
        "s1": (second, "j1"),
        "f2": (first, "block2"),
        "j2": (join, "block2", "f2"),
        "s2": (second, "j2"),
        "f3": (first, "block3"),
        "j3": (join, "block3", "f3"),
        "s3": (second, "j3"),
        "saved": (
            lambda x: call(
                saved_kernel, [shaped(width * slots // 2 // LANES, LANES)], (x,), scratch=fetched(1), name="saved"
            )[0],
            "outputs",
        ),
        "saved_swapped": (core, "saved"),
        "score": (
            lambda got, *blocks: call(
                score_kernel, [shaped(8, LANES, dtype=jnp.float32)], (saved4, got, *blocks),
                scratch=fetched(1), flops=4 * slots * width * tokens, name="score",
            )[0],
            "saved_swapped", "own", "f0", "s0",
        ),
        "part_swapped": (core, "part"),
        "down": (
            lambda a, b: call(
                add_kernel, [jax.ShapeDtypeStruct((rows, width), bf16)], (a, b), name="down", out_space=pltpu.HBM,
                scratch=[pltpu.VMEM((rows, width), bf16), pltpu.SemaphoreType.DMA((len(chunks(width, 4 * LANES)),))],
            )[0],
            "mine", "part_swapped",
        ),
        "route": (
            lambda *scores: call(
                route_kernel,
                [jax.ShapeDtypeStruct((expert_ids.shape[1], tokens), jnp.float32)],
                (expert_ids.T[None, None], *scores),
                scratch=[pltpu.VMEM(expert_ids.shape[::-1], jnp.int32), pltpu.SemaphoreType.DMA],
                name="route",
            )[0],
            "score", "f3", "s3",
        ),
    }
    sums = {
        "t0": ("quarters", "own", "f0", "s0"),
        "t1": ("h1", "near", "f1", "s1"),
        "t2": ("h2", "block2", "f2", "s2"),
        "t3": (*H3, "block3", "f3", "s3"),
    }

    def split(names, values):
        replicas = []
        for n in names:
            many = len(sums[n]) - 3
            hidden = (values[0][0],) if n == "t0" else values[:many]
            replicas.append((hidden, values[many:many + 3]))
            values = values[many + 3:]
        return replicas

    before = None
    for n in TOTALS:
        build = lambda *values, n=n, started=before is not None: add(
            split([n], values[1:] if started else values), values[0] if started else (), name=n
        )
        steps[n] = (build, *([before] if before else []), *sums[n])
        before = n
    late = [n for n in sums if n not in TOTALS]
    for n, experts, out in (("part", (1,), shaped(rows, width)), ("mine", (0,), acc)):
        build = lambda t, *values, n=n, experts=experts, out=out: add(
            split(late, values), [t[w] for w in experts], experts, out, name=n
        )[0]
        steps[n] = (build, before, *(x for m in late for x in sums[m]))
    made = {}

    def get(name):
        if name not in made:
            build, *needs = steps[name]
            values = [get(other) for other in needs]
            earlier = [get(other) for other in AFTER.get(name, ())]
            if earlier:
                values = phase(*values, *earlier)[:len(values)]
            made[name] = build(*values)
        return made[name]

    return (get("down").reshape(1, rows, width), get("route").T)


def fits(mesh, out_grad, expert_ids, gate_weight, saved_hidden, saved_output):
    planes, experts = mesh.shape["dp"], mesh.shape["expert"]
    tokens, width = out_grad.shape[0] // (planes * experts), out_grad.shape[1]
    rest = width % LANES
    return (
        planes == 4
        and experts == 8
        and tokens == LANES
        and 2 * saved_hidden.shape[3] == LANES
        and saved_hidden.shape[4] % (8 * planes) == 0
        and rest > 0
        and rest % 8 == 0
        and LANES % rest == 0
    )


def solution(mesh):
    placed = (
        P(("dp", "expert"), None),
        P(("dp", "expert"), None),
        P(("dp", "expert"), None),
        P("dp", "expert", None, None, None),
        P("dp", "expert", None, None, None),
    )

    def run(*arrays):
        return jax.shard_map(
            planes4 if fits(mesh, *arrays) else general,
            mesh=mesh,
            in_specs=placed,
            out_specs=(P("expert", "dp", None), P(("dp", "expert"), None)),
            check_vma=False,
        )(*arrays)

    return run
```

```python
import functools

import jax
import jax.numpy as jnp
from jax import lax
from jax.experimental import pallas as pl
from jax.experimental.pallas import tpu as pltpu
from jax.sharding import PartitionSpec as P

LANES = 128
META = 16
AFTER = {
    "inside": ("quarters", "saved",),
    "outside": ("saved",),
    "f1": ("across", "saved",),
    "j1": ("s0",),
    "third": ("outside", "saved_swapped",),
    "h3_inner": ("inside", "outside", "across",),
    "f2": ("s0",),
    "h1": ("third",),
    "h2": ("h3_inner",),
    "f3": ("s1",),
    "h3_outer": ("h1", "h2",),
    "j3": ("h1",),
    "turned": ("own",),
}
SCALE, SCALES = 3, {"t2": 0.5, "turned": 2, "t0": 0.5, "own": 40, "saved": 16}
TOTALS = ("t0", "t1", "t2")
H3 = ("h3_inner", "h3_outer")


def slot_numbers(ids, experts, capacity):
    rows = ids.shape[0] * ids.shape[1]
    flat = (ids.reshape(rows, 1) == jnp.arange(experts, dtype=jnp.int32)[None, :]).astype(jnp.int32)
    earlier = jnp.cumsum(flat, axis=0) - flat
    position = jnp.sum(earlier * flat, axis=1).reshape(ids.shape)
    return ids * capacity + position


def general(out_grad, expert_ids, gate_weight, saved_hidden, saved_output):
    tokens_here, width = out_grad.shape
    experts = lax.axis_size("expert")
    capacity = saved_hidden.shape[3]
    hidden_width = saved_hidden.shape[4]
    sources = saved_hidden.shape[2]
    slot = slot_numbers(expert_ids, experts, capacity)
    table = slot[:, :, None] == jnp.arange(experts * capacity, dtype=jnp.int32)[None, None, :]
    occupancy = jnp.sum(table, axis=1).astype(jnp.bfloat16)
    sent = lax.dot_general(
        occupancy, out_grad, (((0,), (0,)), ((), ())), preferred_element_type=jnp.float32
    )
    sent = sent.astype(jnp.bfloat16).reshape(experts, capacity, width)
    gate_slots = jnp.sum(jnp.where(table, gate_weight[:, :, None], jnp.float32(0.0)), axis=(0, 1))
    gate_slots = gate_slots.reshape(experts, capacity)
    arrived, arrived_gate = (
        lax.all_to_all(sent, "expert", split_axis=0, concat_axis=0, tiled=True),
        lax.all_to_all(
            gate_slots.astype(jnp.bfloat16), "expert", split_axis=0, concat_axis=0, tiled=True
        ).astype(gate_slots.dtype),
    )
    scaled = (
        (arrived_gate[:, :, None] * arrived).astype(jnp.bfloat16).reshape(sources * capacity, width)
    )
    hidden = saved_hidden.reshape(sources * capacity, hidden_width)
    own_rows = hidden_width // lax.axis_size("dp")
    down_grad = lax.psum_scatter(
        lax.dot_general(
            hidden, scaled, (((0,), (0,)), ((), ())), preferred_element_type=jnp.float32
        ).astype(jnp.bfloat16),
        "dp",
        scatter_dimension=0,
        tiled=True,
    ).astype(jnp.float32)
    down_grad = down_grad.astype(jnp.bfloat16).reshape(1, own_rows, width)
    outputs = saved_output.reshape(sources, capacity, width)
    returned = lax.all_to_all(outputs, "expert", split_axis=0, concat_axis=0, tiled=True)
    picked = returned.reshape(experts * capacity, width)[slot.reshape(-1)]
    picked = picked.reshape(tokens_here, expert_ids.shape[1], width)
    route_grad = jnp.einsum("tkd,td->tk", picked, out_grad, preferred_element_type=jnp.float32)
    return (down_grad, route_grad)


def pack_kernel(grad_ref, ids_ref, gate_ref, out_ref, ids, gate, sems):
    width, tokens = grad_ref.shape[2:]
    copies = [
        pltpu.make_async_copy(ids_ref.at[0, 0], ids, sems.at[0]),
        pltpu.make_async_copy(gate_ref.at[0, 0], gate, sems.at[1]),
        pltpu.make_async_copy(grad_ref.at[0, 0], out_ref.at[:width], sems.at[2]),
    ]
    for copy in copies:
        copy.start()
    copies[0].wait()
    copies[1].wait()
    expert = lax.broadcasted_iota(jnp.int32, (META // 2, tokens), 0)
    dense = jnp.zeros((META // 2, tokens), jnp.float32)
    for k in range(ids.shape[0]):
        dense = dense + jnp.where(expert == ids[k:k + 1, :], gate[k:k + 1, :], 0.0)
    high = dense.astype(jnp.bfloat16).astype(jnp.float32)
    out_ref[width:, :] = jnp.concatenate([high, dense - high], axis=0).astype(jnp.bfloat16)
    copies[2].wait()


def fetch(source, target, sems, cores):
    copies = [
        [pltpu.make_async_copy(source.at[c, core], target.at[c, n], sems.at[c, n]) for n, core in enumerate(cores)]
        for c in range(source.shape[0])
    ]
    for chip in copies:
        for copy in chip:
            copy.start()
    return copies


def arrive(copies):
    for chip in copies:
        for copy in chip:
            copy.wait()


def stacked(ref, n, cols, chips):
    return jnp.concatenate([ref[c, n, :, cols] for c in chips], axis=0)


def turn_kernel(hidden_ref, keep_ref, leave_ref, here, sems):
    core = lax.axis_index("expert") & 1
    copies = fetch(hidden_ref, here, sems, (core, 1 - core))
    width, pair = here.shape[3], 2 * here.shape[2]
    for c in range(0, here.shape[0], 2):
        arrive(copies[c:c + 2])
        to = slice(c // 2 * pair, (c // 2 + 1) * pair)
        for a in range(0, width, LANES):
            cols = slice(a, min(a + LANES, width))
            keep_ref[cols, to] = stacked(here, 0, cols, (c, c + 1)).T
            leave_ref[cols, to] = stacked(here, 1, cols, (c, c + 1)).T


def quarter_kernel(keep_ref, got_ref, *rest):
    outs, scratch = rest[:-1], rest[-1]
    planes, rows, half = len(outs), outs[0].shape[0], keep_ref.shape[1]
    for q in range(planes):
        scratch[q, :, :half] = keep_ref[q * rows:(q + 1) * rows, :]
        scratch[q, :, half:] = got_ref[q * rows:(q + 1) * rows, :]
    for o in range(planes):
        outs[o][...] = scratch[lax.axis_index("dp") ^ o]


def saved_kernel(saved_ref, out_ref, here, sems):
    arrive(fetch(saved_ref, here, sems, (1 - (lax.axis_index("expert") & 1),)))
    chips = range(here.shape[0])
    rows, width = here.shape[0] * here.shape[2], here.shape[3]
    full, rest = width // LANES, width % LANES
    for j in range(full):
        out_ref[j * rows:(j + 1) * rows, :] = stacked(here, 0, slice(j * LANES, (j + 1) * LANES), chips)
    tail = stacked(here, 0, slice(full * LANES, width), chips).astype(jnp.float32)
    step = rows * rest // LANES
    out_ref[full * rows:, :] = jnp.concatenate(
        [tail[a * step:(a + 1) * step] for a in range(LANES // rest)], axis=1
    ).astype(jnp.bfloat16)


def choose_kernel(inner_ref, outer_ref, *refs):
    out_ref = refs[-1]
    rows = inner_ref.shape[0]
    plane = lax.axis_index("dp")
    middle = jnp.logical_or(plane == 1, plane == 2)

    @pl.when(middle)
    def _():
        out_ref[:rows, :] = inner_ref[...]

    @pl.when(jnp.logical_not(middle))
    def _():
        out_ref[:rows, :] = outer_ref[...]

    if len(refs) > 1:
        score = refs[0][...]
        high = score.astype(jnp.bfloat16).astype(jnp.float32)
        out_ref[rows:, :] = jnp.concatenate([high, score - high], axis=0).astype(jnp.bfloat16)


def join_kernel(a_ref, b_ref, out_ref):
    out_ref[0] = a_ref[...]
    out_ref[1] = b_ref[...]


def block_tables(blocks, width):
    me = lax.axis_index("expert")
    core, chip = me & 1, me >> 1
    offsets = [0, 1 + core, 2 - core, 3]
    rows = lax.broadcasted_iota(jnp.int32, (META, LANES), 0)
    metas = [ref[width:width + META, :].astype(jnp.float32) for ref in blocks]
    gates = []
    for expert in (me, me ^ 1):
        picked = jnp.logical_or(rows == expert, rows == expert + META // 2)
        gates += [jnp.sum(jnp.where(picked, meta, 0.0), axis=0, keepdims=True) for meta in metas]
    gates = jnp.concatenate(gates, axis=0)
    routed = gates > 0.0
    before = lax.broadcasted_iota(jnp.int32, (LANES, LANES), 0) < lax.broadcasted_iota(jnp.int32, (LANES, LANES), 1)
    earlier = jnp.dot(
        routed.astype(jnp.bfloat16), before.astype(jnp.bfloat16), preferred_element_type=jnp.float32
    ).astype(jnp.int32)
    position = jnp.where(routed, earlier, -LANES * LANES)
    number = len(blocks)
    out = []
    for w in range(2):
        gate = jnp.concatenate([gates[w * number + n:w * number + n + 1] for n in range(number)], axis=1)
        place = jnp.concatenate(
            [position[w * number + n:w * number + n + 1] + (chip ^ offsets[n]) * (LANES // 2) for n in range(number)],
            axis=1,
        )
        out.append((gate, place))
    return out


def chosen(place, slots):
    return lax.broadcasted_iota(jnp.int32, (slots, place.shape[1]), 0) == place


def gather_hidden(hidden, table):
    gate, place = table
    placed = jnp.dot(
        hidden, chosen(place, hidden.shape[1]).astype(jnp.bfloat16), preferred_element_type=jnp.float32
    )
    return (placed * gate).astype(jnp.bfloat16)


def chunks(width, step=2 * LANES):
    return [(a, min(a + step, width)) for a in range(0, width, step)]


def tokens_of(blocks, a, b):
    return jnp.concatenate([ref[a:b, :] for ref in blocks], axis=1)


def four(refs):
    own, first, pair = refs
    return [own, first, pair.at[0], pair.at[1]]


def sum_kernel(choices, experts, started, *refs):
    number = len(experts)
    outs, refs = refs[-number:], refs[:-number]
    accs, refs = (refs[:number], refs[number:]) if started else ((), refs)
    rows, width = outs[0].shape
    plane = lax.axis_index("dp")
    middle = jnp.logical_or(plane == 1, plane == 2)
    replicas = []
    for many in choices:
        hidden_refs, blocks, refs = refs[:many], four(refs[many:many + 3]), refs[many + 3:]
        tables = block_tables(blocks, width)
        half = hidden_refs[0].shape[1] // 2
        hidden = []
        for w in experts:
            parts = [ref[:, w * half:(w + 1) * half] for ref in hidden_refs]
            hidden.append(gather_hidden(parts[0] if many == 1 else jnp.where(middle, *parts), tables[w]))
        replicas.append((hidden[0] if number == 1 else jnp.concatenate(hidden, axis=0), blocks))
    for a, b in chunks(width):
        total = None
        for hidden, blocks in replicas:
            product = lax.dot_general(
                hidden, tokens_of(blocks, a, b), (((1,), (1,)), ((), ())), preferred_element_type=jnp.float32
            )
            total = product if total is None else total + product
        for w, out_ref in enumerate(outs):
            value = total[w * rows:(w + 1) * rows]
            if started:
                value = value + accs[w][:, a:b]
            out_ref[:, a:b] = value.astype(out_ref.dtype)


def score_kernel(saved_ref, got_ref, *refs):
    blocks, (score_ref, here, sems) = four(refs[:-3]), refs[-3:]
    copies = fetch(saved_ref, here, sems, (lax.axis_index("expert") & 1,))
    chips = range(here.shape[0])
    rows, width = here.shape[0] * here.shape[2], here.shape[3]
    tables = block_tables(blocks, width)
    arrive(copies)
    full, rest = width // LANES, width % LANES
    total = jnp.zeros((2 * rows, len(blocks) * LANES), jnp.float32)
    for a, b in chunks(width):
        pieces = []
        for j in range(a // LANES, -(-b // LANES)):
            if j < full:
                pieces.append(got_ref[j * rows:(j + 1) * rows, :])
            else:
                tail = got_ref[full * rows:, :]
                pieces.append(
                    jnp.concatenate([tail[:, n * rest:(n + 1) * rest] for n in range(LANES // rest)], axis=0)
                )
        theirs = pieces[0] if len(pieces) == 1 else jnp.concatenate(pieces, axis=1)
        saved = jnp.concatenate([stacked(here, 0, slice(a, b), chips), theirs], axis=0)
        total = total + jnp.dot(saved, tokens_of(blocks, a, b), preferred_element_type=jnp.float32)
    scores = []
    for w in range(2):
        row = jnp.sum(
            jnp.where(chosen(tables[w][1], rows), total[w * rows:(w + 1) * rows], 0.0), axis=0, keepdims=True
        )
        scores += [row[:, n * LANES:(n + 1) * LANES] for n in range(len(blocks))]
    score_ref[...] = jnp.concatenate(scores, axis=0)


def route_kernel(ids_ref, score_ref, first_ref, pair_ref, out_ref, ids, sem):
    copy = pltpu.make_async_copy(ids_ref.at[0, 0], ids, sem)
    copy.start()
    half = META // 2
    parts = [score_ref[...]]
    for ref in (first_ref, pair_ref.at[0], pair_ref.at[1]):
        sent = ref[ref.shape[0] - META:, :].astype(jnp.float32)
        parts.append(sent[:half] + sent[half:])
    me = lax.axis_index("expert")
    core = me & 1
    offsets = [0, 2 + 2 * core, 4 - 2 * core, 6]
    copy.wait()
    wanted = ids[...] ^ me
    total = jnp.zeros(wanted.shape, jnp.float32)
    for w in range(2):
        for n, part in enumerate(parts):
            total = total + jnp.where(wanted == offsets[n] ^ w, part[4 * w + n:4 * w + n + 1], 0.0)
    out_ref[...] = total


def add_kernel(a_ref, b_ref, out_ref, total, sems):
    copies = []
    for n, (a, b) in enumerate(chunks(a_ref.shape[1], 4 * LANES)):
        total[:, a:b] = (a_ref[:, a:b] + b_ref[:, a:b].astype(jnp.float32)).astype(total.dtype)
        copies.append(pltpu.make_async_copy(total.at[:, a:b], out_ref.at[:, a:b], sems.at[n]))
        copies[-1].start()
    for copy in copies:
        copy.wait()


def call(kernel, outs, args, scratch=(), flops=0, limit=8, aliases=None, name=None, out_space=pltpu.VMEM):
    vmem, hbm = (pl.BlockSpec(memory_space=space) for space in (pltpu.VMEM, pltpu.HBM))
    moved = sum(a.size * a.dtype.itemsize for a in args)
    scale = SCALES.get(name, SCALE)
    specs, operands = [], []
    for a in args:
        specs.append(hbm if a.ndim == 4 else vmem)
        if a.ndim > 1:
            a = pltpu.with_memory_space_constraint(a, pltpu.HBM if a.ndim == 4 else pltpu.VMEM)
        operands.append(a)
    return pl.pallas_call(
        kernel,
        out_shape=outs,
        in_specs=specs,
        out_specs=[pl.BlockSpec(memory_space=out_space)] * len(outs),
        scratch_shapes=list(scratch),
        input_output_aliases=aliases or {},
        compiler_params=pltpu.CompilerParams(vmem_limit_bytes=limit * 1024 * 1024),
        cost_estimate=pl.CostEstimate(flops=int(scale * flops), bytes_accessed=int(scale * moved), transcendentals=0),
    )(*operands)


def phase(*values):
    return lax.optimization_barrier(values)


def after(value, *earlier):
    return phase(value, *earlier)[0]


def planes4(out_grad, expert_ids, gate_weight, saved_hidden, saved_output):
    tokens, width = out_grad.shape
    hidden_width = saved_hidden.shape[4]
    sources, capacity = saved_hidden.shape[2:4]
    slots = sources * capacity
    planes = lax.axis_size("dp")
    rows = hidden_width // planes
    bf16 = jnp.bfloat16

    def permute(name, target):
        return lambda x: lax.ppermute(x, name, [(i, target(i)) for i in range(lax.axis_size(name))])

    core = permute("expert", lambda i: i ^ 1)
    first = permute("expert", lambda i: i ^ (4 if i & 1 else 2))
    second = permute("expert", lambda i: i ^ (2 if i & 1 else 4))
    far1, far2, far3 = (permute("dp", lambda i, o=o: i ^ o) for o in (1, 2, 3))
    inner = lambda x: lax.ppermute(x, "dp", [(1, 2), (2, 1)])
    outer = lambda x: lax.ppermute(x, "dp", [(0, 3), (3, 0)])
    outward = lambda x: lax.ppermute(x, "dp", [(1, 0), (2, 3)])
    hidden4 = saved_hidden.reshape(sources // 2, 2, capacity, hidden_width)
    saved4 = saved_output.reshape(sources // 2, 2, capacity, width)

    def shaped(*shape, dtype=bf16):
        return pltpu.VMEM(shape, dtype)

    def fetched(cores):
        return [
            pltpu.VMEM((sources // 2, cores, capacity, width), bf16),
            pltpu.SemaphoreType.DMA((sources // 2, cores)),
        ]

    acc = shaped(rows, width, dtype=jnp.float32)
    flops = 4 * rows * width * 4 * tokens

    def add(replicas, totals=(), experts=(0, 1), out=acc, name=None):
        arrays = [x for hidden, blocks in replicas for x in (*hidden, *blocks)]
        return call(
            functools.partial(sum_kernel, [len(hidden) for hidden, blocks in replicas], experts, bool(totals)),
            [out] * len(experts),
            (*totals, *arrays), flops=flops * len(replicas) * len(experts) // 2, name=name,
            aliases={n: n for n in range(len(totals))} if out is acc else None,
        )

    def choose(inner_block, outer_block, *score):
        extra = META if score else 0
        return call(
            choose_kernel, [shaped(width + META + extra, tokens)], (inner_block, outer_block, *score)
        )[0]

    def join(a, b):
        return call(join_kernel, [shaped(2, *a.shape)], (a, b))[0]

    steps = {
        "hidden": (lambda: hidden4,),
        "outputs": (lambda: saved4,),
        "own": (
            lambda: call(
                pack_kernel,
                [shaped(width + META, tokens)],
                tuple(x.T[None, None] for x in (out_grad, expert_ids, gate_weight)),
                scratch=[
                    pltpu.VMEM(expert_ids.shape[::-1], jnp.int32),
                    pltpu.VMEM(gate_weight.shape[::-1], jnp.float32),
                    pltpu.SemaphoreType.DMA((3,)),
                ],
                name="own",
            )[0],
        ),
        "turned": (
            lambda x: call(
                turn_kernel, [shaped(hidden_width, slots // 2)] * 2, (x,), scratch=fetched(2), name="turned"
            ),
            "hidden",
        ),
        "swapped": (lambda t: core(t[1]), "turned"),
        "quarters": (
            lambda t, got: call(
                quarter_kernel,
                [shaped(rows, slots)] * planes,
                (t[0], got),
                scratch=[pltpu.VMEM((planes, rows, slots), bf16)],
                name="quarters",
            ),
            "turned", "swapped",
        ),
        "h1": (lambda h: far1(h[1]), "quarters"),
        "h2": (lambda h: far2(h[2]), "quarters"),
        "h3": (lambda h: far3(h[3]), "quarters"),
        "h3_inner": (lambda h: inner(h[3]), "quarters"),
        "h3_outer": (lambda h: outer(h[3]), "quarters"),
        "near": (far1, "own"),
        "across": (inner, "own"),
        "inside": (inner, "near"),
        "outside": (outward, "across"),
        "third": (outward, "inside"),
        "block2": (choose, "inside", "outside"),
        "block3": (choose, "across", "third", "score"),
        "f0": (first, "own"),
        "j0": (join, "own", "f0"),
        "s0": (second, "j0"),
        "f1": (first, "near"),
        "j1": (join, "near", "f1"),
        "s1": (second, "j1"),
        "f2": (first, "block2"),
        "j2": (join, "block2", "f2"),
        "s2": (second, "j2"),
        "f3": (first, "block3"),
        "j3": (join, "block3", "f3"),
        "s3": (second, "j3"),
        "saved": (
            lambda x: call(
                saved_kernel, [shaped(width * slots // 2 // LANES, LANES)], (x,), scratch=fetched(1), name="saved"
            )[0],
            "outputs",
        ),
        "saved_swapped": (core, "saved"),
        "score": (
            lambda got, *blocks: call(
                score_kernel, [shaped(8, LANES, dtype=jnp.float32)], (saved4, got, *blocks),
                scratch=fetched(1), flops=4 * slots * width * tokens, name="score",
            )[0],
            "saved_swapped", "own", "f0", "s0",
        ),
        "part_swapped": (core, "part"),
        "down": (
            lambda a, b: call(
                add_kernel, [jax.ShapeDtypeStruct((rows, width), bf16)], (a, b), name="down", out_space=pltpu.HBM,
                scratch=[pltpu.VMEM((rows, width), bf16), pltpu.SemaphoreType.DMA((len(chunks(width, 4 * LANES)),))],
            )[0],
            "mine", "part_swapped",
        ),
        "route": (
            lambda *scores: call(
                route_kernel,
                [jax.ShapeDtypeStruct((expert_ids.shape[1], tokens), jnp.float32)],
                (expert_ids.T[None, None], *scores),
                scratch=[pltpu.VMEM(expert_ids.shape[::-1], jnp.int32), pltpu.SemaphoreType.DMA],
                name="route",
            )[0],
            "score", "f3", "s3",
        ),
    }
    sums = {
        "t0": ("quarters", "own", "f0", "s0"),
        "t1": ("h1", "near", "f1", "s1"),
        "t2": ("h2", "block2", "f2", "s2"),
        "t3": (*H3, "block3", "f3", "s3"),
    }

    def split(names, values):
        replicas = []
        for n in names:
            many = len(sums[n]) - 3
            hidden = (values[0][0],) if n == "t0" else values[:many]
            replicas.append((hidden, values[many:many + 3]))
            values = values[many + 3:]
        return replicas

    before = None
    for n in TOTALS:
        build = lambda *values, n=n, started=before is not None: add(
            split([n], values[1:] if started else values), values[0] if started else (), name=n
        )
        steps[n] = (build, *([before] if before else []), *sums[n])
        before = n
    late = [n for n in sums if n not in TOTALS]
    for n, experts, out in (("part", (1,), shaped(rows, width)), ("mine", (0,), acc)):
        build = lambda t, *values, n=n, experts=experts, out=out: add(
            split(late, values), [t[w] for w in experts], experts, out, name=n
        )[0]
        steps[n] = (build, before, *(x for m in late for x in sums[m]))
    made = {}

    def get(name):
        if name not in made:
            build, *needs = steps[name]
            values = [get(other) for other in needs]
            earlier = [get(other) for other in AFTER.get(name, ())]
            if earlier:
                values = phase(*values, *earlier)[:len(values)]
            made[name] = build(*values)
        return made[name]

    return (get("down").reshape(1, rows, width), get("route").T)


def fits(mesh, out_grad, expert_ids, gate_weight, saved_hidden, saved_output):
    planes, experts = mesh.shape["dp"], mesh.shape["expert"]
    tokens, width = out_grad.shape[0] // (planes * experts), out_grad.shape[1]
    rest = width % LANES
    return (
        planes == 4
        and experts == 8
        and tokens == LANES
        and 2 * saved_hidden.shape[3] == LANES
        and saved_hidden.shape[4] % (8 * planes) == 0
        and rest > 0
        and rest % 8 == 0
        and LANES % rest == 0
    )


def solution(mesh):
    placed = (
        P(("dp", "expert"), None),
        P(("dp", "expert"), None),
        P(("dp", "expert"), None),
        P("dp", "expert", None, None, None),
        P("dp", "expert", None, None, None),
    )

    def run(*arrays):
        return jax.shard_map(
            planes4 if fits(mesh, *arrays) else general,
            mesh=mesh,
            in_specs=placed,
            out_specs=(P("expert", "dp", None), P(("dp", "expert"), None)),
            check_vma=False,
        )(*arrays)

    return run
```
